512 devices in a mesh: pair: 64 (over x_lo, z, core), band: 8 (over y, x_hi).
Axes of the slice: x: 4 (x_hi: 2, x_lo: 2; x = x_hi * 2 + x_lo), y: 4, z: 16, core: 2. Of those that a mesh axis runs over, the one named last changes fastest.
Arguments:
- spectra: bfloat16 [2, 64, 512, 2048], P(None, None, 'pair', 'band'), may hold values from -40 to 40
- validity: int32 [64, 512], P(None, 'pair'), may hold values 0 or 1
Outputs:
- correlations: float32 [7, 512, 8, 128], P(None, 'pair', 'band')
The draws below stay inside these ranges and needn't reach their ends.
All inputs are finite; a program needn't handle non-finite values. No bound on the sum of `validity` on one device may be relied on, other than what follows from the above.
Results may differ from the reference program's by a relative error of at most 0.004.
Values may be sent and summed in bfloat16 or wider, within the bound.
No kernel may reach another device: no remote copies, remote signals or barrier semaphores. Data moves between devices by JAX's collectives and lax.ppermute only.
A program may use at most 64 MiB of HBM per device.

```python
import math
import jax
import jax.numpy as jnp
from jax import lax

S_DEV = 8
WIN = 64
ROUNDS = 6
BAND_BINS = 128
LAGS = 128
NBINS = 2048
STATIONS = 512
N_PAIR = 64


def draw_spectra(key, part):
    key = jax.random.fold_in(key, 1)
    keys = jax.random.split(key, 3)
    shape = (2, WIN, STATIONS, NBINS)
    base = jax.random.normal(keys[0], shape, jnp.float32)
    span = math.log(10.0)
    row_scale = jnp.exp(jax.random.uniform(keys[1], (1, WIN, STATIONS, 1), jnp.float32, 0.0, span))
    bin_scale = jnp.exp(jax.random.uniform(keys[2], (1, 1, 1, NBINS), jnp.float32, math.log(0.3), math.log(3.0)))
    return jnp.clip(base * row_scale * bin_scale, -40.0, 40.0).astype(jnp.bfloat16)


def plant(entries, stream_key, least, largest):
    shape = entries.shape
    index_at = [jax.random.randint(jax.random.fold_in(stream_key, axis), (), 0, shape[axis]) for axis in range(len(shape))]
    entries = entries.at[tuple(index_at)].set(least)
    longest = shape.index(max(shape))
    index_at[longest] = (index_at[longest] + 1) % shape[longest]
    return entries.at[tuple(index_at)].set(largest)


def setup_inputs(seed: int = 0) -> dict:
    arg_keys = jax.random.split(jax.random.key(seed), 3)
    return {
        "spectra": draw_spectra(jax.random.fold_in(arg_keys[2], 71), 0),
        "validity": plant((jax.random.randint(arg_keys[1], (WIN, STATIONS), 0, 4) < 3).astype(jnp.int32), jax.random.fold_in(arg_keys[1], 1), 0, 1),
    }


def whiten(spectra, validity):
    values = spectra.astype(jnp.float32)
    magnitude = jnp.sqrt(values[0] * values[0] + values[1] * values[1])
    win_count, station_count, bin_count = magnitude.shape
    grouped = magnitude.reshape(win_count, station_count, bin_count // BAND_BINS, BAND_BINS)
    band_mean = lax.optimization_barrier(jnp.mean(grouped, axis=-1, keepdims=True))
    factor = jnp.broadcast_to(1.0 / (band_mean + 1e-06), grouped.shape).reshape(win_count, station_count, bin_count)
    factor = factor * validity.astype(jnp.float32)[:, :, None]
    return (values * factor[None]).astype(jnp.bfloat16)

def lag_table(first_bin, bin_count):
    freq = first_bin + jnp.arange(bin_count, dtype=jnp.int32)
    offsets = jnp.arange(LAGS, dtype=jnp.int32) - LAGS // 2
    wrapped = freq[:, None] * offsets[None, :] % (2 * NBINS)
    phase_arg = math.pi * wrapped.astype(jnp.float32) / NBINS
    return (jnp.cos(phase_arg), jnp.sin(phase_arg))

def cross_block(left, right):
    left_f = left.astype(jnp.float32)
    right_f = right.astype(jnp.float32)
    hp = lax.Precision.HIGHEST
    real_part = jnp.einsum('cwpf,cwqf->pqf', left_f, right_f, precision=hp)
    imag_part = jnp.einsum('wpf,wqf->pqf', left_f[0], right_f[1], precision=hp) - jnp.einsum('wpf,wqf->pqf', left_f[1], right_f[0], precision=hp)
    scale = 1.0 / math.sqrt(WIN)
    return (real_part * scale, imag_part * scale)

def reference(spectra, validity):
    whitened = whiten(spectra, validity)
    cos_table, sin_table = lag_table(0, NBINS)
    blocks = whitened.reshape(2, WIN, N_PAIR, S_DEV, NBINS)
    off_diag = 1.0 - jnp.eye(S_DEV, dtype=jnp.float32)
    hp = lax.Precision.HIGHEST

    def per_block(block_no):
        own_block = lax.dynamic_index_in_dim(blocks, block_no, 2, keepdims=False)
        results = []
        for round_no in range(ROUNDS + 1):
            other = ((block_no + round_no) % N_PAIR).astype(jnp.int32)
            partner = lax.dynamic_index_in_dim(blocks, other, 2, keepdims=False)
            real_part, imag_part = cross_block(own_block, partner)
            if round_no == 0:
                real_part = real_part * off_diag[:, :, None]
                imag_part = imag_part * off_diag[:, :, None]
            lagged = jnp.einsum('pqf,fl->pql', real_part, cos_table, precision=hp) - jnp.einsum('pqf,fl->pql', imag_part, sin_table, precision=hp)
            results.append(lagged / math.sqrt(NBINS))
        return jnp.stack(results)
    mapped = lax.map(per_block, jnp.arange(N_PAIR, dtype=jnp.int32))
    return mapped.transpose(1, 0, 2, 3, 4).reshape(ROUNDS + 1, N_PAIR * S_DEV, S_DEV, LAGS)
```

```python
import math

import jax
import jax.numpy as jnp
from jax import lax
from jax.experimental import pallas as pl
from jax.experimental.pallas import tpu as pltpu
from jax.sharding import PartitionSpec as P

WIN = 64
ROUNDS = 6
BAND_BINS = 128
LAGS = 128
NBINS = 2048
S_DEV = 8
LINES = 2 * WIN
GROUP = 8
GROUPS = BAND_BINS // GROUP
PIECE = S_DEV * GROUP
ROWS = 2 * PIECE
VMEM_LIMIT = 48 * 1024 * 1024


def core_index():
    return lax.rem(lax.axis_index("pair"), 2)


def whiten_kernel(spectra_ref, valid_ref, same_ref, cross_ref, lines_ref):
    core = core_index()
    values = spectra_ref[...].astype(jnp.float32)
    magnitude = jnp.sqrt(values[0] * values[0] + values[1] * values[1])
    for half in range(2):
        cut = slice(half * BAND_BINS, (half + 1) * BAND_BINS)
        band_mean = jnp.sum(magnitude[:, :, cut], axis=-1, keepdims=True) * (1.0 / BAND_BINS)
        factor = 1.0 / (band_mean + 1e-06)
        scaled = values[:, :, :, cut] * factor[None]
        lines_ref[half] = scaled.reshape(LINES * S_DEV, BAND_BINS)
    usable = valid_ref[...].astype(jnp.float32)
    usable = jnp.concatenate([usable, usable], axis=1)
    for out_ref, half in ((same_ref, core), (cross_ref, 1 - core)):
        for pair in range(S_DEV // 2):
            parts = []
            for station in (2 * pair, 2 * pair + 1):
                lines = lines_ref[half, pl.ds(station, LINES, stride=S_DEV), :]
                turned = lines.T * usable[station : station + 1, :]
                parts.append(turned.reshape(GROUPS, GROUP, LINES))
            both = jnp.concatenate(parts, axis=1).astype(jnp.bfloat16)
            out_ref[:, pair * 2 * GROUP : (pair + 1) * 2 * GROUP, :] = both


def whiten(spectra, valid):
    piece = jax.ShapeDtypeStruct((GROUPS, PIECE, LINES), jnp.bfloat16)
    return pl.pallas_call(
        whiten_kernel,
        out_shape=(piece, piece),
        in_specs=[pl.BlockSpec(memory_space=pltpu.VMEM)] * 2,
        out_specs=[pl.BlockSpec(memory_space=pltpu.VMEM)] * 2,
        scratch_shapes=[pltpu.VMEM((2, LINES * S_DEV, BAND_BINS), jnp.float32)],
        compiler_params=pltpu.CompilerParams(vmem_limit_bytes=VMEM_LIMIT),
    )(spectra, valid)


def cross_kernel(late, *refs):
    count = 3 if late else 2
    piece_refs = refs[: 2 * count]
    table_ref, out_ref, held, left, turned, sems = refs[2 * count :]
    core = core_index()
    copies = []
    for index in range(count):
        for which in range(2):
            parity = core if which == 0 else 1 - core
            start = pl.multiple_of(parity * PIECE, PIECE)
            copy = pltpu.make_async_copy(
                piece_refs[2 * index + which],
                held.at[index, :, pl.ds(start, PIECE), :],
                sems.at[2 * index + which],
            )
            copy.start()
            copies.append(copy)
    for copy in copies:
        copy.wait()
    if late:
        pairs = ((2 * core, 2 - 2 * core), (1 + core, 2 - core))
    else:
        pairs = ((0, 0), (1 - core, core))

    row = lax.broadcasted_iota(jnp.int32, (ROWS, ROWS), 0)
    col = lax.broadcasted_iota(jnp.int32, (ROWS, ROWS), 1)
    swap_rows = (col == (row % 16) * GROUP + row // 16).astype(jnp.bfloat16)
    lane = lax.broadcasted_iota(jnp.int32, (16, ROWS), 1)
    sign = jnp.where(lax.broadcasted_iota(jnp.int32, (ROWS, LINES), 1) < WIN, -1.0, 1.0)

    for number, (p_side, q_side) in enumerate(pairs):
        for group in range(GROUPS):
            plain = jnp.dot(
                swap_rows, held[p_side, group], preferred_element_type=jnp.float32
            )
            flipped = pltpu.roll(plain, WIN, 1) * sign
            left[number, group, :ROWS, :] = plain.astype(jnp.bfloat16)
            left[number, group, ROWS:, :] = flipped.astype(jnp.bfloat16)

    for group in range(GROUPS):
        picked = []
        for number, (p_side, q_side) in enumerate(pairs):
            full = lax.dot_general(
                left[number, group],
                held[q_side, group],
                (((1,), (1,)), ((), ())),
                preferred_element_type=jnp.float32,
            )
            for part in range(2):
                total = jnp.zeros((16, ROWS), jnp.float32)
                for line in range(GROUP):
                    first = part * ROWS + line * 16
                    total = jnp.where(
                        lane % GROUP == line, full[first : first + 16, :], total
                    )
                picked.append(total)
        stacked = jnp.concatenate([picked[0], picked[2], picked[1], picked[3]], axis=0)
        turned[:, group * GROUP : (group + 1) * GROUP, :] = stacked.T.reshape(16, GROUP, 64)

    table = table_ref[...]
    for q in range(16):
        lines = turned[q].T
        lagged = jnp.dot(
            lines, table, precision=lax.Precision.HIGHEST, preferred_element_type=jnp.float32
        )
        summed = lagged[:32, :LAGS] + lagged[32:, LAGS:]
        for number in range(2):
            for parity in range(2):
                first = number * 16 + parity * 8
                out_ref[parity * 8 + q % 8, number * 2 + q // 8] = summed[first : first + 8, :]


def cross(late, pieces, table):
    count = len(pieces) // 2
    return pl.pallas_call(
        lambda *refs: cross_kernel(late, *refs),
        out_shape=jax.ShapeDtypeStruct((16, 4, S_DEV, LAGS), jnp.float32),
        in_specs=[pl.BlockSpec(memory_space=pl.ANY)] * (2 * count)
        + [pl.BlockSpec(memory_space=pltpu.VMEM)],
        out_specs=pl.BlockSpec(memory_space=pltpu.VMEM),
        scratch_shapes=[
            pltpu.VMEM((count, GROUPS, ROWS, LINES), jnp.bfloat16),
            pltpu.VMEM((2, GROUPS, 2 * ROWS, LINES), jnp.bfloat16),
            pltpu.VMEM((16, BAND_BINS, 64), jnp.float32),
            pltpu.SemaphoreType.DMA((2 * count,)),
        ],
        compiler_params=pltpu.CompilerParams(vmem_limit_bytes=VMEM_LIMIT),
        cost_estimate=pl.CostEstimate(
            flops=2 * 2 * GROUPS * 3 * ROWS * ROWS * LINES,
            bytes_accessed=count * 524288 + 262144,
            transcendentals=0,
        ),
    )(*pieces, table)


def gather_kernel(early_ref, late_ref, home_ref, one_ref, two_ref):
    def summed(ref, half):
        total = ref[half * 8]
        for index in range(1, 8):
            total = total + ref[half * 8 + index]
        return total

    early = [summed(early_ref, half) for half in range(2)]
    late = [summed(late_ref, half) for half in range(2)]
    home_ref[0:2] = early[0][0:2] + early[1][0:2]
    home_ref[2:4] = early[1][2:4]
    home_ref[4:6] = late[0][0:2]
    one_ref[0:2] = early[0][2:4]
    one_ref[2:4] = late[0][2:4]
    two_ref[...] = late[1]


def gather(early, late):
    def shape(count):
        return jax.ShapeDtypeStruct((count, S_DEV, LAGS), jnp.float32)

    return pl.pallas_call(
        gather_kernel,
        out_shape=(shape(6), shape(4), shape(4)),
        compiler_params=pltpu.CompilerParams(vmem_limit_bytes=VMEM_LIMIT),
    )(early, late)


def finish_kernel(home_ref, one_ref, two_ref, out_ref, slots):
    core = core_index()
    band = lax.axis_index("band")
    scale = 1.0 / (math.sqrt(WIN) * math.sqrt(NBINS))
    slots[0:2] = home_ref[0:2]
    slots[2:4] = home_ref[2:4] + one_ref[0:2]
    slots[4:6] = home_ref[4:6] + two_ref[0:2]
    slots[6:8] = one_ref[2:4] + two_ref[2:4]
    for round_no in range(ROUNDS + 1):
        value = slots[round_no + core] * scale
        if round_no == 0:
            row = lax.broadcasted_iota(jnp.int32, (S_DEV, LAGS), 0)
            value = jnp.where(row == band, 0.0, value)
        out_ref[round_no] = value


def finish(home, one, two):
    return pl.pallas_call(
        finish_kernel,
        out_shape=jax.ShapeDtypeStruct((ROUNDS + 1, S_DEV, LAGS), jnp.float32),
        scratch_shapes=[pltpu.VMEM((8, S_DEV, LAGS), jnp.float32)],
        compiler_params=pltpu.CompilerParams(vmem_limit_bytes=VMEM_LIMIT),
    )(home, one, two)


def send(value, steps, other=False):
    count = lax.axis_size("pair")
    pairs = []
    for source in range(count):
        core = source % 2
        target = source - core + 2 * steps[core] + (1 - core if other else core)
        pairs.append((source, target % count))
    return lax.ppermute(value, "pair", pairs)


def exchange(value):
    bands = lax.axis_size("band")
    groups = [
        [(2 * chip + core) * bands + band for core in range(2) for band in range(bands)]
        for chip in range(lax.axis_size("pair") // 2)
    ]
    return lax.all_to_all(
        value, ("pair", "band"), 0, 0, tiled=True, axis_index_groups=groups
    )


def lag_table(first_bin):
    freq = first_bin + jnp.arange(BAND_BINS, dtype=jnp.int32)
    offsets = jnp.arange(LAGS, dtype=jnp.int32) - LAGS // 2
    wrapped = freq[:, None] * offsets[None, :] % (2 * NBINS)
    phase = math.pi * wrapped.astype(jnp.float32) / NBINS
    return jnp.concatenate([jnp.cos(phase), -jnp.sin(phase)], axis=1)


def body(spectra, validity):
    same, other = whiten(spectra, validity.T)
    core = core_index()
    first_bin = (lax.axis_index("band") * 2 + core) * BAND_BINS
    table = lag_table(first_bin)
    near_same = send(same, (1, -1))
    near_other = send(other, (-1, 1), other=True)
    own_other = send(other, (0, 0), other=True)
    far_same = send(same, (-2, 2))
    far_other = send(other, (2, -2), other=True)
    own = [same, own_other]
    near = [near_same, near_other]
    far = [far_same, far_other]
    early = exchange(cross(False, own + near, table))
    late = exchange(cross(True, own + near + far, table))
    home, one, two = gather(early, late)
    one = send(one, (-1, -1))
    two = send(two, (-2, -2))
    return finish(home, one, two).reshape(ROUNDS + 1, S_DEV, 1, LAGS)


def solution(mesh):
    return jax.shard_map(
        body,
        mesh=mesh,
        in_specs=(P(None, None, "pair", "band"), P(None, "pair")),
        out_specs=P(None, "pair", "band", None),
        check_vma=False,
    )
```

```python
import math

import jax
import jax.numpy as jnp
from jax import lax
from jax.experimental import pallas as pl
from jax.experimental.pallas import tpu as pltpu
from jax.sharding import PartitionSpec as P

WIN = 64
ROUNDS = 6
BAND_BINS = 128
LAGS = 128
NBINS = 2048
S_DEV = 8
LINES = 2 * WIN
GROUP = 8
GROUPS = BAND_BINS // GROUP
PIECE = S_DEV * GROUP
ROWS = 2 * PIECE
CHUNKS = 4
WHITEN_LIMIT = 52 * 1024 * 1024
VMEM_LIMIT = 48 * 1024 * 1024


def core_index():
    return lax.rem(lax.axis_index("pair"), 2)


def whiten_kernel(spectra_hbm, valid_hbm, *refs):
    out_refs, (raw, valid, lines_ref, sems) = refs[:6], refs[6:]
    core = core_index()
    step = WIN // CHUNKS
    copies = []
    for chunk in range(CHUNKS):
        span = pl.ds(chunk * step, step)
        copies.append(
            pltpu.make_async_copy(spectra_hbm.at[:, span], raw.at[:, span], sems.at[chunk])
        )
        copies[-1].start()
    copies.append(pltpu.make_async_copy(valid_hbm, valid, sems.at[CHUNKS]))
    copies[-1].start()
    for chunk in range(CHUNKS):
        copies[chunk].wait()
        values = raw[:, chunk * step : (chunk + 1) * step].astype(jnp.float32)
        magnitude = jnp.sqrt(values[0] * values[0] + values[1] * values[1])
        for half in range(2):
            cut = slice(half * BAND_BINS, (half + 1) * BAND_BINS)
            band_mean = jnp.sum(magnitude[:, :, cut], axis=-1, keepdims=True) * (1.0 / BAND_BINS)
            factor = 1.0 / (band_mean + 1e-06)
            scaled = values[:, :, :, cut] * factor[None]
            for part in range(2):
                first = (part * WIN + chunk * step) * S_DEV
                lines_ref[half, first : first + step * S_DEV, :] = scaled[part].reshape(
                    step * S_DEV, BAND_BINS
                )
    copies[CHUNKS].wait()
    usable = valid[...].astype(jnp.float32)
    usable = jnp.concatenate([usable, usable], axis=1)
    for index, half in enumerate((core, 1 - core)):
        for pair in range(S_DEV // 2):
            parts = []
            for station in (2 * pair, 2 * pair + 1):
                lines = lines_ref[half, pl.ds(station, LINES, stride=S_DEV), :]
                turned = lines.T * usable[station : station + 1, :]
                parts.append(turned.reshape(GROUPS, GROUP, LINES))
            both = jnp.concatenate(parts, axis=1).astype(jnp.bfloat16)
            for out_ref in out_refs[index::2]:
                out_ref[:, pair * 2 * GROUP : (pair + 1) * 2 * GROUP, :] = both


def whiten(spectra, valid):
    piece = jax.ShapeDtypeStruct((GROUPS, PIECE, LINES), jnp.bfloat16)
    return pl.pallas_call(
        whiten_kernel,
        out_shape=(piece,) * 6,
        in_specs=[pl.BlockSpec(memory_space=pl.ANY)] * 2,
        out_specs=[pl.BlockSpec(memory_space=pltpu.VMEM)] * 6,
        scratch_shapes=[
            pltpu.VMEM((2, WIN, S_DEV, 2 * BAND_BINS), jnp.bfloat16),
            pltpu.VMEM((S_DEV, WIN), jnp.int32),
            pltpu.VMEM((2, LINES * S_DEV, BAND_BINS), jnp.float32),
            pltpu.SemaphoreType.DMA((CHUNKS + 1,)),
        ],
        compiler_params=pltpu.CompilerParams(vmem_limit_bytes=WHITEN_LIMIT),
    )(spectra, valid)


def cross_kernel(late, *refs):
    count = 3 if late else 2
    piece_refs = refs[: 2 * count]
    if late:
        table_ref, early_ref, out_ref, held, left, turned, sems = refs[2 * count :]
        out_ref[...] = early_ref[...]
    else:
        table_ref, out_ref, held, left, turned, sems = refs[2 * count :]
    core = core_index()
    copies = []
    for index in range(count):
        for which in range(2):
            parity = core if which == 0 else 1 - core
            start = pl.multiple_of(parity * PIECE, PIECE)
            copy = pltpu.make_async_copy(
                piece_refs[2 * index + which],
                held.at[index, :, pl.ds(start, PIECE), :],
                sems.at[2 * index + which],
            )
            copy.start()
            copies.append(copy)
    for copy in copies:
        copy.wait()
    if late:
        pairs = ((1, 1 + core, 2 - core), (3, 1 - core, core))
    else:
        pairs = ((0, 1, 1), (2, 1 - core, core))

    row = lax.broadcasted_iota(jnp.int32, (ROWS, ROWS), 0)
    col = lax.broadcasted_iota(jnp.int32, (ROWS, ROWS), 1)
    swap_rows = (col == (row % 16) * GROUP + row // 16).astype(jnp.bfloat16)
    lane = lax.broadcasted_iota(jnp.int32, (16, ROWS), 1)
    sign = jnp.where(lax.broadcasted_iota(jnp.int32, (ROWS, LINES), 1) < WIN, -1.0, 1.0)

    for number, (_, p_side, q_side) in enumerate(pairs):
        for group in range(GROUPS):
            plain = jnp.dot(
                swap_rows, held[p_side, group], preferred_element_type=jnp.float32
            )
            flipped = pltpu.roll(plain, WIN, 1) * sign
            left[number, group, :ROWS, :] = plain.astype(jnp.bfloat16)
            left[number, group, ROWS:, :] = flipped.astype(jnp.bfloat16)

    for group in range(GROUPS):
        picked = []
        for number, (_, p_side, q_side) in enumerate(pairs):
            full = lax.dot_general(
                left[number, group],
                held[q_side, group],
                (((1,), (1,)), ((), ())),
                preferred_element_type=jnp.float32,
            )
            for part in range(2):
                total = jnp.zeros((16, ROWS), jnp.float32)
                for line in range(GROUP):
                    first = part * ROWS + line * 16
                    total = jnp.where(
                        lane % GROUP == line, full[first : first + 16, :], total
                    )
                picked.append(total)
        stacked = jnp.concatenate([picked[0], picked[2], picked[1], picked[3]], axis=0)
        turned[:, group * GROUP : (group + 1) * GROUP, :] = stacked.T.reshape(16, GROUP, 64)

    table_high = table_ref[...].astype(jnp.bfloat16)
    table_low = (table_ref[...] - table_high.astype(jnp.float32)).astype(jnp.bfloat16)
    for first_q in range(0, 16, 4):
        lines = jnp.concatenate([turned[first_q + step].T for step in range(4)], axis=0)
        high = lines.astype(jnp.bfloat16)
        low = (lines - high.astype(jnp.float32)).astype(jnp.bfloat16)
        lagged = (
            jnp.dot(high, table_high, preferred_element_type=jnp.float32)
            + jnp.dot(low, table_high, preferred_element_type=jnp.float32)
            + jnp.dot(high, table_low, preferred_element_type=jnp.float32)
        )
        for step in range(4):
            q = first_q + step
            part = lagged[step * 64 : (step + 1) * 64]
            summed = part[:32, :LAGS] + part[32:, LAGS:]
            for number, (apart, _, _) in enumerate(pairs):
                for parity in range(2):
                    round_no = 2 * apart + q // 8 - parity
                    if 0 <= round_no <= ROUNDS:
                        first = number * 16 + parity * 8
                        out_ref[parity * 8 + q % 8, round_no] = summed[first : first + 8, :]


def cross(pieces, table, early=None):
    count = len(pieces) // 2
    late = [] if early is None else [early]
    return pl.pallas_call(
        lambda *refs: cross_kernel(bool(late), *refs),
        out_shape=jax.ShapeDtypeStruct((16, ROUNDS + 1, S_DEV, LAGS), jnp.float32),
        in_specs=[pl.BlockSpec(memory_space=pl.ANY)] * (2 * count)
        + [pl.BlockSpec(memory_space=pltpu.VMEM)] * (1 + len(late)),
        out_specs=pl.BlockSpec(memory_space=pltpu.VMEM),
        scratch_shapes=[
            pltpu.VMEM((count, GROUPS, ROWS, LINES), jnp.bfloat16),
            pltpu.VMEM((2, GROUPS, 2 * ROWS, LINES), jnp.bfloat16),
            pltpu.VMEM((16, BAND_BINS, 64), jnp.float32),
            pltpu.SemaphoreType.DMA((2 * count,)),
        ],
        compiler_params=pltpu.CompilerParams(vmem_limit_bytes=VMEM_LIMIT),
        cost_estimate=pl.CostEstimate(
            flops=2 * 2 * GROUPS * 3 * ROWS * ROWS * LINES,
            bytes_accessed=count * 524288 + 262144,
            transcendentals=0,
        ),
    )(*pieces, table, *late)


def gather_kernel(parts_ref, home_ref, one_ref, two_ref, slots):
    core = core_index()
    for half in range(2):
        total = parts_ref[half * 8]
        for index in range(1, 8):
            total = total + parts_ref[half * 8 + index]
        slots[half, pl.ds(core, ROUNDS + 1)] = total
        slots[half, 7 - 7 * core] = jnp.zeros((S_DEV, LAGS), jnp.float32)
    home_ref[0:2] = slots[0, 0:2] + slots[1, 0:2]
    home_ref[2:4] = slots[1, 2:4]
    home_ref[4:6] = slots[0, 4:6]
    one_ref[0:2] = slots[0, 2:4]
    one_ref[2:4] = slots[0, 6:8]
    two_ref[...] = slots[1, 4:8]


def gather(parts):
    def shape(count):
        return jax.ShapeDtypeStruct((count, S_DEV, LAGS), jnp.float32)

    return pl.pallas_call(
        gather_kernel,
        out_shape=(shape(6), shape(4), shape(4)),
        scratch_shapes=[pltpu.VMEM((2, 8, S_DEV, LAGS), jnp.float32)],
        compiler_params=pltpu.CompilerParams(vmem_limit_bytes=VMEM_LIMIT),
    )(parts)


def finish_kernel(home_ref, one_ref, two_ref, out_ref, slots):
    core = core_index()
    band = lax.axis_index("band")
    scale = 1.0 / (math.sqrt(WIN) * math.sqrt(NBINS))
    slots[0:2] = home_ref[0:2]
    slots[2:4] = home_ref[2:4] + one_ref[0:2]
    slots[4:6] = home_ref[4:6] + two_ref[0:2]
    slots[6:8] = one_ref[2:4] + two_ref[2:4]
    for round_no in range(ROUNDS + 1):
        value = slots[round_no + core] * scale
        if round_no == 0:
            row = lax.broadcasted_iota(jnp.int32, (S_DEV, LAGS), 0)
            value = jnp.where(row == band, 0.0, value)
        out_ref[round_no] = value


def finish(home, one, two):
    return pl.pallas_call(
        finish_kernel,
        out_shape=jax.ShapeDtypeStruct((ROUNDS + 1, S_DEV, LAGS), jnp.float32),
        scratch_shapes=[pltpu.VMEM((8, S_DEV, LAGS), jnp.float32)],
        compiler_params=pltpu.CompilerParams(vmem_limit_bytes=VMEM_LIMIT),
    )(home, one, two)


def send(value, steps, other=False):
    count = lax.axis_size("pair")
    pairs = []
    for source in range(count):
        core = source % 2
        target = source - core + 2 * steps[core] + (1 - core if other else core)
        pairs.append((source, target % count))
    return lax.ppermute(value, "pair", pairs)


def exchange(value):
    bands = lax.axis_size("band")
    groups = [
        [(2 * chip + core) * bands + band for core in range(2) for band in range(bands)]
        for chip in range(lax.axis_size("pair") // 2)
    ]
    return lax.all_to_all(
        value, ("pair", "band"), 0, 0, tiled=True, axis_index_groups=groups
    )


def lag_table(first_bin):
    freq = first_bin + jnp.arange(BAND_BINS, dtype=jnp.int32)
    offsets = jnp.arange(LAGS, dtype=jnp.int32) - LAGS // 2
    wrapped = freq[:, None] * offsets[None, :] % (2 * NBINS)
    phase = math.pi * wrapped.astype(jnp.float32) / NBINS
    return jnp.concatenate([jnp.cos(phase), -jnp.sin(phase)], axis=1)


def body(spectra, validity):
    far_same, far_other, own_same, own_other, near_same, near_other = whiten(spectra, validity.T)
    first_bin = (lax.axis_index("band") * 2 + core_index()) * BAND_BINS
    table = lag_table(first_bin)
    far = [send(far_same, (-2, 2)), send(far_other, (2, -2), other=True)]
    own = [own_same, send(own_other, (0, 0), other=True)]
    near = [send(near_same, (1, -1)), send(near_other, (-1, 1), other=True)]
    early = cross(far + own, table)
    late = cross(far + near + own, table, early)
    home, one, two = gather(exchange(late))
    one = send(one, (-1, -1))
    two = send(two, (-2, -2))
    return finish(home, one, two).reshape(ROUNDS + 1, S_DEV, 1, LAGS)


def solution(mesh):
    return jax.shard_map(
        body,
        mesh=mesh,
        in_specs=(P(None, None, "pair", "band"), P(None, "pair")),
        out_specs=P(None, "pair", "band", None),
        check_vma=False,
    )
```

```python
import math

import jax
import jax.numpy as jnp
from jax import lax
from jax.experimental import pallas as pl
from jax.experimental.pallas import tpu as pltpu
from jax.sharding import PartitionSpec as P

WIN = 64
ROUNDS = 6
BAND_BINS = 128
LAGS = 128
NBINS = 2048
S_DEV = 8
LINES = 2 * WIN
GROUP = 8
GROUPS = BAND_BINS // GROUP
PIECE = S_DEV * GROUP
ROWS = 2 * PIECE
CHUNKS = 4
WHITEN_LIMIT = 52 * 1024 * 1024
VMEM_LIMIT = 48 * 1024 * 1024


def core_index():
    return lax.rem(lax.axis_index("pair"), 2)


def whiten_kernel(spectra_hbm, valid_hbm, *refs):
    out_refs, (raw, valid, lines_ref, sems) = refs[:6], refs[6:]
    core = core_index()
    step = WIN // CHUNKS
    copies = []
    for chunk in range(CHUNKS):
        span = pl.ds(chunk * step, step)
        copies.append(
            pltpu.make_async_copy(spectra_hbm.at[:, span], raw.at[:, span], sems.at[chunk])
        )
        copies[-1].start()
    copies.append(pltpu.make_async_copy(valid_hbm, valid, sems.at[CHUNKS]))
    copies[-1].start()
    for chunk in range(CHUNKS):
        copies[chunk].wait()
        values = raw[:, chunk * step : (chunk + 1) * step].astype(jnp.float32)
        magnitude = jnp.sqrt(values[0] * values[0] + values[1] * values[1])
        for half in range(2):
            cut = slice(half * BAND_BINS, (half + 1) * BAND_BINS)
            band_mean = jnp.sum(magnitude[:, :, cut], axis=-1, keepdims=True) * (1.0 / BAND_BINS)
            factor = 1.0 / (band_mean + 1e-06)
            scaled = values[:, :, :, cut] * factor[None]
            for part in range(2):
                first = (part * WIN + chunk * step) * S_DEV
                lines_ref[half, first : first + step * S_DEV, :] = scaled[part].reshape(
                    step * S_DEV, BAND_BINS
                )
    copies[CHUNKS].wait()
    usable = valid[...].astype(jnp.float32)
    usable = jnp.concatenate([usable, usable], axis=1)
    for index, half in enumerate((core, 1 - core)):
        for pair in range(S_DEV // 2):
            parts = []
            for station in (2 * pair, 2 * pair + 1):
                lines = lines_ref[half, pl.ds(station, LINES, stride=S_DEV), :]
                turned = lines.T * usable[station : station + 1, :]
                parts.append(turned.reshape(GROUPS, GROUP, LINES))
            both = jnp.concatenate(parts, axis=1).astype(jnp.bfloat16)
            for out_ref in out_refs[index::2]:
                out_ref[:, pair * 2 * GROUP : (pair + 1) * 2 * GROUP, :] = both


def whiten(spectra, valid):
    piece = jax.ShapeDtypeStruct((GROUPS, PIECE, LINES), jnp.bfloat16)
    return pl.pallas_call(
        whiten_kernel,
        out_shape=(piece,) * 6,
        in_specs=[pl.BlockSpec(memory_space=pl.ANY)] * 2,
        out_specs=[pl.BlockSpec(memory_space=pltpu.VMEM)] * 6,
        scratch_shapes=[
            pltpu.VMEM((2, WIN, S_DEV, 2 * BAND_BINS), jnp.bfloat16),
            pltpu.VMEM((S_DEV, WIN), jnp.int32),
            pltpu.VMEM((2, LINES * S_DEV, BAND_BINS), jnp.float32),
            pltpu.SemaphoreType.DMA((CHUNKS + 1,)),
        ],
        compiler_params=pltpu.CompilerParams(vmem_limit_bytes=WHITEN_LIMIT),
    )(spectra, valid)


FAR, NEAR, OWN = 0, 1, 2


def cross_kernel(places, *refs):
    late = (FAR, 0) in places
    piece_refs = refs[: len(places)]
    if late:
        table_ref, early_ref, out_ref, held, left, turned, sems = refs[len(places) :]
        out_ref[:, :2] = early_ref[...]
    else:
        table_ref, out_ref, held, left, turned, sems = refs[len(places) :]
    core = core_index()
    copies = []
    for index, (chip, other) in enumerate(places):
        parity = 1 - core if other else core
        start = pl.multiple_of(parity * PIECE, PIECE)
        copy = pltpu.make_async_copy(
            piece_refs[index], held.at[chip, :, pl.ds(start, PIECE), :], sems.at[index]
        )
        copy.start()
        copies.append(copy)
    for copy in copies:
        copy.wait()
    pairs = ((OWN, FAR), (NEAR, FAR)) if late else ((OWN, OWN), (NEAR, OWN))

    row = lax.broadcasted_iota(jnp.int32, (ROWS, ROWS), 0)
    col = lax.broadcasted_iota(jnp.int32, (ROWS, ROWS), 1)
    swap_rows = (col == (row % 16) * GROUP + row // 16).astype(jnp.bfloat16)
    lane = lax.broadcasted_iota(jnp.int32, (16, ROWS), 1)
    sign = jnp.where(lax.broadcasted_iota(jnp.int32, (ROWS, LINES), 1) < WIN, -1.0, 1.0)

    for number, (p_side, q_side) in enumerate(pairs):
        for group in range(GROUPS):
            plain = jnp.dot(
                swap_rows, held[p_side, group], preferred_element_type=jnp.float32
            )
            flipped = pltpu.roll(plain, WIN, 1) * sign
            left[number, group, :ROWS, :] = plain.astype(jnp.bfloat16)
            left[number, group, ROWS:, :] = flipped.astype(jnp.bfloat16)

    for group in range(GROUPS):
        picked = []
        for number, (p_side, q_side) in enumerate(pairs):
            full = lax.dot_general(
                left[number, group],
                held[q_side, group],
                (((1,), (1,)), ((), ())),
                preferred_element_type=jnp.float32,
            )
            for part in range(2):
                total = jnp.zeros((16, ROWS), jnp.float32)
                for line in range(GROUP):
                    first = part * ROWS + line * 16
                    total = jnp.where(
                        lane % GROUP == line, full[first : first + 16, :], total
                    )
                picked.append(total)
        stacked = jnp.concatenate([picked[0], picked[2], picked[1], picked[3]], axis=0)
        turned[:, group * GROUP : (group + 1) * GROUP, :] = stacked.T.reshape(16, GROUP, 64)

    table_high = table_ref[...].astype(jnp.bfloat16)
    table_low = (table_ref[...] - table_high.astype(jnp.float32)).astype(jnp.bfloat16)
    for first_q in range(0, 8, 2):
        stations = (first_q, first_q + 8, first_q + 1, first_q + 9)
        lines = jnp.concatenate([turned[q].T for q in stations], axis=0)
        high = lines.astype(jnp.bfloat16)
        low = (lines - high.astype(jnp.float32)).astype(jnp.bfloat16)
        lagged = (
            jnp.dot(high, table_high, preferred_element_type=jnp.float32)
            + jnp.dot(low, table_high, preferred_element_type=jnp.float32)
            + jnp.dot(high, table_low, preferred_element_type=jnp.float32)
        )
        for step in range(2):
            sums = []
            for q_parity in range(2):
                part = lagged[(2 * step + q_parity) * 64 : (2 * step + q_parity + 1) * 64]
                sums.append(part[:32, :LAGS] + part[32:, LAGS:])
            for number in range(2):
                for parity in range(2):
                    cut = slice(number * 16 + parity * 8, number * 16 + parity * 8 + 8)
                    out_ref[parity * 8 + first_q + step, (2 if late else 0) + number] = (
                        jnp.concatenate([sums[0][cut], sums[1][cut]], axis=0).astype(
                            jnp.bfloat16
                        )
                    )


def cross(pieces, table, early=None):
    late = [] if early is None else [early]
    places = tuple(pieces)
    return pl.pallas_call(
        lambda *refs: cross_kernel(places, *refs),
        out_shape=jax.ShapeDtypeStruct((16, 4 if late else 2, 16, LAGS), jnp.bfloat16),
        in_specs=[pl.BlockSpec(memory_space=pl.ANY)] * len(places)
        + [pl.BlockSpec(memory_space=pltpu.VMEM)] * (1 + len(late)),
        out_specs=pl.BlockSpec(memory_space=pltpu.VMEM),
        scratch_shapes=[
            pltpu.VMEM((3, GROUPS, ROWS, LINES), jnp.bfloat16),
            pltpu.VMEM((2, GROUPS, 2 * ROWS, LINES), jnp.bfloat16),
            pltpu.VMEM((16, BAND_BINS, 64), jnp.float32),
            pltpu.SemaphoreType.DMA((len(places),)),
        ],
        compiler_params=pltpu.CompilerParams(vmem_limit_bytes=VMEM_LIMIT),
        cost_estimate=pl.CostEstimate(
            flops=2 * 2 * GROUPS * 3 * ROWS * ROWS * LINES,
            bytes_accessed=len(places) * 262144 + 262144,
            transcendentals=0,
        ),
    )(*pieces.values(), table, *late)


def gather_kernel(parts_ref, home_ref, away_ref):
    total = parts_ref[0].astype(jnp.float32)
    for index in range(1, 16):
        total = total + parts_ref[index].astype(jnp.float32)
    home_ref[0] = total[0]
    home_ref[1] = total[2]
    away_ref[0] = total[1]
    away_ref[1] = total[3]


def gather(parts):
    half = jax.ShapeDtypeStruct((2, 16, LAGS), jnp.float32)
    return pl.pallas_call(
        gather_kernel,
        out_shape=(half, half),
        compiler_params=pltpu.CompilerParams(vmem_limit_bytes=VMEM_LIMIT),
    )(parts)


def finish_kernel(home_ref, away_ref, out_ref, slots):
    core = core_index()
    band = lax.axis_index("band")
    scale = 1.0 / (math.sqrt(WIN) * math.sqrt(NBINS))
    slots[0:16] = home_ref[0]
    slots[16:32] = away_ref[0]
    slots[32:48] = home_ref[1]
    slots[48:64] = away_ref[1]
    for round_no in range(ROUNDS + 1):
        first = pl.multiple_of((round_no + core) * S_DEV, S_DEV)
        value = slots[pl.ds(first, S_DEV), :] * scale
        if round_no == 0:
            row = lax.broadcasted_iota(jnp.int32, (S_DEV, LAGS), 0)
            value = jnp.where(row == band, 0.0, value)
        out_ref[round_no] = value


def finish(home, away):
    return pl.pallas_call(
        finish_kernel,
        out_shape=jax.ShapeDtypeStruct((ROUNDS + 1, S_DEV, LAGS), jnp.float32),
        scratch_shapes=[pltpu.VMEM((8 * S_DEV, LAGS), jnp.float32)],
        compiler_params=pltpu.CompilerParams(vmem_limit_bytes=VMEM_LIMIT),
    )(home, away)


def send(value, chips, other=False):
    count = lax.axis_size("pair")
    pairs = []
    for source in range(count):
        target = source + 2 * chips
        if other:
            target = target + 1 - 2 * (source % 2)
        pairs.append((source, target % count))
    return lax.ppermute(value, "pair", pairs)


def exchange(value):
    bands = lax.axis_size("band")
    groups = [
        [(2 * chip + core) * bands + band for core in range(2) for band in range(bands)]
        for chip in range(lax.axis_size("pair") // 2)
    ]
    return lax.all_to_all(
        value, ("pair", "band"), 0, 0, tiled=True, axis_index_groups=groups
    )


def lag_table(first_bin):
    freq = first_bin + jnp.arange(BAND_BINS, dtype=jnp.int32)
    offsets = jnp.arange(LAGS, dtype=jnp.int32) - LAGS // 2
    wrapped = freq[:, None] * offsets[None, :] % (2 * NBINS)
    phase = math.pi * wrapped.astype(jnp.float32) / NBINS
    return jnp.concatenate([jnp.cos(phase), -jnp.sin(phase)], axis=1)


def body(spectra, validity):
    far_same, far_other, own_same, own_other, near_same, near_other = whiten(spectra, validity.T)
    first_bin = (lax.axis_index("band") * 2 + core_index()) * BAND_BINS
    table = lag_table(first_bin)
    pieces = {
        (FAR, 0): send(far_same, -2),
        (NEAR, 0): send(near_same, 1),
        (FAR, 1): send(far_other, -2, other=True),
        (NEAR, 1): send(near_other, 1, other=True),
        (OWN, 0): own_same,
        (OWN, 1): send(own_other, 0, other=True),
    }
    early = cross({place: piece for place, piece in pieces.items() if place[0] != FAR}, table)
    late = cross(pieces, table, early)
    home, away = gather(exchange(late))
    return finish(home, send(away, -1)).reshape(ROUNDS + 1, S_DEV, 1, LAGS)


def solution(mesh):
    return jax.shard_map(
        body,
        mesh=mesh,
        in_specs=(P(None, None, "pair", "band"), P(None, "pair")),
        out_specs=P(None, "pair", "band", None),
        check_vma=False,
    )
```

```python
import math

import jax
import jax.numpy as jnp
from jax import lax
from jax.experimental import pallas as pl
from jax.experimental.pallas import tpu as pltpu
from jax.sharding import PartitionSpec as P

WIN = 64
ROUNDS = 6
BAND_BINS = 128
LAGS = 128
NBINS = 2048
S_DEV = 8
LINES = 2 * WIN
GROUP = 8
GROUPS = BAND_BINS // GROUP
PIECE = S_DEV * GROUP
ROWS = 2 * PIECE
CHUNKS = 2
WHITEN_LIMIT = 52 * 1024 * 1024
VMEM_LIMIT = 24 * 1024 * 1024


def core_index():
    return lax.rem(lax.axis_index("pair"), 2)


def whiten_kernel(spectra_hbm, valid_hbm, *refs):
    out_refs, (raw, valid, lines_ref, sems) = refs[:6], refs[6:]
    core = core_index()
    step = WIN // CHUNKS
    copies = []
    for chunk in range(CHUNKS):
        span = pl.ds(chunk * step, step)
        copies.append(
            pltpu.make_async_copy(spectra_hbm.at[:, span], raw.at[:, span], sems.at[chunk])
        )
        copies[-1].start()
    copies.append(pltpu.make_async_copy(valid_hbm, valid, sems.at[CHUNKS]))
    copies[-1].start()
    for chunk in range(CHUNKS):
        copies[chunk].wait()
        values = raw[:, chunk * step : (chunk + 1) * step].astype(jnp.float32)
        magnitude = jnp.sqrt(values[0] * values[0] + values[1] * values[1])
        for half in range(2):
            cut = slice(half * BAND_BINS, (half + 1) * BAND_BINS)
            band_mean = jnp.sum(magnitude[:, :, cut], axis=-1, keepdims=True) * (1.0 / BAND_BINS)
            factor = 1.0 / (band_mean + 1e-06)
            scaled = values[:, :, :, cut] * factor[None]
            for part in range(2):
                first = (part * WIN + chunk * step) * S_DEV
                lines_ref[half, first : first + step * S_DEV, :] = scaled[part].reshape(
                    step * S_DEV, BAND_BINS
                )
    copies[CHUNKS].wait()
    usable = valid[...].astype(jnp.float32)
    usable = jnp.concatenate([usable, usable], axis=1)
    for index, half in enumerate((core, 1 - core)):
        for pair in range(S_DEV // 2):
            parts = []
            for station in (2 * pair, 2 * pair + 1):
                lines = lines_ref[half, pl.ds(station, LINES, stride=S_DEV), :]
                turned = lines.T * usable[station : station + 1, :]
                parts.append(turned.reshape(GROUPS, GROUP, LINES))
            both = jnp.concatenate(parts, axis=1).astype(jnp.bfloat16)
            for out_ref in out_refs[index::2]:
                out_ref[:, pair * 2 * GROUP : (pair + 1) * 2 * GROUP, :] = both


def whiten(spectra, valid):
    piece = jax.ShapeDtypeStruct((GROUPS, PIECE, LINES), jnp.bfloat16)
    return pl.pallas_call(
        whiten_kernel,
        out_shape=(piece,) * 6,
        in_specs=[pl.BlockSpec(memory_space=pl.ANY)] * 2,
        out_specs=[pl.BlockSpec(memory_space=pltpu.VMEM)] * 6,
        scratch_shapes=[
            pltpu.VMEM((2, WIN, S_DEV, 2 * BAND_BINS), jnp.bfloat16),
            pltpu.VMEM((S_DEV, WIN), jnp.int32),
            pltpu.VMEM((2, LINES * S_DEV, BAND_BINS), jnp.float32),
            pltpu.SemaphoreType.DMA((CHUNKS + 1,)),
        ],
        compiler_params=pltpu.CompilerParams(vmem_limit_bytes=WHITEN_LIMIT),
    )(spectra, valid)


FAR, NEAR, OWN = 0, 1, 2


def cross_kernel(places, *refs):
    late = (FAR, 0) in places
    piece_refs = refs[: len(places)]
    if late:
        table_ref, early_ref, left, out_ref, held, turned, sems = refs[len(places) :]
        out_ref[:, :2] = early_ref[...]
    else:
        table_ref, out_ref, left, held, turned, sems = refs[len(places) :]
    core = core_index()
    copies = []
    for index, (chip, other) in enumerate(places):
        if late and chip != FAR:
            continue
        parity = 1 - core if other else core
        start = pl.multiple_of(parity * PIECE, PIECE)
        copy = pltpu.make_async_copy(
            piece_refs[index], held.at[chip, :, pl.ds(start, PIECE), :], sems.at[index]
        )
        copy.start()
        copies.append(copy)
    for copy in copies:
        copy.wait()
    pairs = ((OWN, FAR), (NEAR, FAR)) if late else ((OWN, OWN), (NEAR, OWN))

    row = lax.broadcasted_iota(jnp.int32, (ROWS, ROWS), 0)
    col = lax.broadcasted_iota(jnp.int32, (ROWS, ROWS), 1)
    swap_rows = (col == (row % 16) * GROUP + row // 16).astype(jnp.bfloat16)
    lane = lax.broadcasted_iota(jnp.int32, (16, ROWS), 1)
    sign = jnp.where(lax.broadcasted_iota(jnp.int32, (ROWS, LINES), 1) < WIN, -1.0, 1.0)

    for number, (p_side, q_side) in enumerate(() if late else pairs):
        for group in range(GROUPS):
            plain = jnp.dot(
                swap_rows, held[p_side, group], preferred_element_type=jnp.float32
            )
            flipped = pltpu.roll(plain, WIN, 1) * sign
            left[number, group, :ROWS, :] = plain.astype(jnp.bfloat16)
            left[number, group, ROWS:, :] = flipped.astype(jnp.bfloat16)

    for group in range(GROUPS):
        picked = []
        for number, (p_side, q_side) in enumerate(pairs):
            full = lax.dot_general(
                left[number, group],
                held[q_side, group],
                (((1,), (1,)), ((), ())),
                preferred_element_type=jnp.float32,
            )
            for part in range(2):
                total = jnp.zeros((16, ROWS), jnp.float32)
                for line in range(GROUP):
                    first = part * ROWS + line * 16
                    total = jnp.where(
                        lane % GROUP == line, full[first : first + 16, :], total
                    )
                picked.append(total)
        stacked = jnp.concatenate([picked[0], picked[2], picked[1], picked[3]], axis=0)
        turned[:, group * GROUP : (group + 1) * GROUP, :] = stacked.T.reshape(16, GROUP, 64)

    table_high = table_ref[...].astype(jnp.bfloat16)
    table_low = (table_ref[...] - table_high.astype(jnp.float32)).astype(jnp.bfloat16)
    for first_q in range(0, 8, 2):
        stations = (first_q, first_q + 8, first_q + 1, first_q + 9)
        lines = jnp.concatenate([turned[q].T for q in stations], axis=0)
        high = lines.astype(jnp.bfloat16)
        low = (lines - high.astype(jnp.float32)).astype(jnp.bfloat16)
        lagged = (
            jnp.dot(high, table_high, preferred_element_type=jnp.float32)
            + jnp.dot(low, table_high, preferred_element_type=jnp.float32)
            + jnp.dot(high, table_low, preferred_element_type=jnp.float32)
        )
        for step in range(2):
            sums = []
            for q_parity in range(2):
                part = lagged[(2 * step + q_parity) * 64 : (2 * step + q_parity + 1) * 64]
                sums.append(part[:32, :LAGS] + part[32:, LAGS:])
            for number in range(2):
                for parity in range(2):
                    cut = slice(number * 16 + parity * 8, number * 16 + parity * 8 + 8)
                    out_ref[parity * 8 + first_q + step, (2 if late else 0) + number] = (
                        jnp.concatenate([sums[0][cut], sums[1][cut]], axis=0).astype(
                            jnp.bfloat16
                        )
                    )


def cross(pieces, table, *early):
    places = tuple(pieces)
    shape = jax.ShapeDtypeStruct((16, 4 if early else 2, 16, LAGS), jnp.bfloat16)
    left = jax.ShapeDtypeStruct((2, GROUPS, 2 * ROWS, LINES), jnp.bfloat16)
    return pl.pallas_call(
        lambda *refs: cross_kernel(places, *refs),
        out_shape=shape if early else (shape, left),
        in_specs=[pl.BlockSpec(memory_space=pl.ANY)] * len(places)
        + [pl.BlockSpec(memory_space=pltpu.VMEM)] * (1 + len(early)),
        scratch_shapes=[
            pltpu.VMEM((3, GROUPS, ROWS, LINES), jnp.bfloat16),
            pltpu.VMEM((16, BAND_BINS, 64), jnp.float32),
            pltpu.SemaphoreType.DMA((len(places),)),
        ],
        compiler_params=pltpu.CompilerParams(vmem_limit_bytes=VMEM_LIMIT),
        cost_estimate=pl.CostEstimate(
            flops=2 * 2 * GROUPS * 3 * ROWS * ROWS * LINES,
            bytes_accessed=len(places) * 262144 + 262144,
            transcendentals=0,
        ),
    )(*pieces.values(), table, *early)


def gather_kernel(parts_ref, home_ref, away_ref):
    total = parts_ref[0].astype(jnp.float32)
    for index in range(1, 16):
        total = total + parts_ref[index].astype(jnp.float32)
    home_ref[0] = total[0]
    home_ref[1] = total[2]
    away_ref[0] = total[1]
    away_ref[1] = total[3]


def gather(parts):
    half = jax.ShapeDtypeStruct((2, 16, LAGS), jnp.float32)
    return pl.pallas_call(
        gather_kernel,
        out_shape=(half, half),
        compiler_params=pltpu.CompilerParams(vmem_limit_bytes=VMEM_LIMIT),
    )(parts)


def finish_kernel(home_ref, away_ref, out_ref, slots):
    core = core_index()
    band = lax.axis_index("band")
    scale = 1.0 / (math.sqrt(WIN) * math.sqrt(NBINS))
    slots[0:16] = home_ref[0]
    slots[16:32] = away_ref[0]
    slots[32:48] = home_ref[1]
    slots[48:64] = away_ref[1]
    for round_no in range(ROUNDS + 1):
        first = pl.multiple_of((round_no + core) * S_DEV, S_DEV)
        value = slots[pl.ds(first, S_DEV), :] * scale
        if round_no == 0:
            row = lax.broadcasted_iota(jnp.int32, (S_DEV, LAGS), 0)
            value = jnp.where(row == band, 0.0, value)
        out_ref[round_no] = value


def finish(home, away):
    return pl.pallas_call(
        finish_kernel,
        out_shape=jax.ShapeDtypeStruct((ROUNDS + 1, S_DEV, LAGS), jnp.float32),
        scratch_shapes=[pltpu.VMEM((8 * S_DEV, LAGS), jnp.float32)],
        compiler_params=pltpu.CompilerParams(vmem_limit_bytes=VMEM_LIMIT),
    )(home, away)


def send(value, chips, other=False):
    count = lax.axis_size("pair")
    pairs = []
    for source in range(count):
        target = source + 2 * chips
        if other:
            target = target + 1 - 2 * (source % 2)
        pairs.append((source, target % count))
    return lax.ppermute(value, "pair", pairs)


def exchange(value):
    bands = lax.axis_size("band")
    groups = [
        [(2 * chip + core) * bands + band for core in range(2) for band in range(bands)]
        for chip in range(lax.axis_size("pair") // 2)
    ]
    return lax.all_to_all(
        value, ("pair", "band"), 0, 0, tiled=True, axis_index_groups=groups
    )


def lag_table(first_bin):
    freq = first_bin + jnp.arange(BAND_BINS, dtype=jnp.int32)
    offsets = jnp.arange(LAGS, dtype=jnp.int32) - LAGS // 2
    wrapped = freq[:, None] * offsets[None, :] % (2 * NBINS)
    phase = math.pi * wrapped.astype(jnp.float32) / NBINS
    return jnp.concatenate([jnp.cos(phase), -jnp.sin(phase)], axis=1)


def body(spectra, validity):
    far_same, far_other, own_same, own_other, near_same, near_other = whiten(spectra, validity.T)
    first_bin = (lax.axis_index("band") * 2 + core_index()) * BAND_BINS
    table = lag_table(first_bin)
    first = {(FAR, 0): send(far_same, -2)}
    middle = {(NEAR, 0): send(near_same, 1)}
    second = {(FAR, 1): send(far_other, -2, other=True)}
    last = {
        (NEAR, 1): send(near_other, 1, other=True),
        (OWN, 0): own_same,
        (OWN, 1): send(own_other, 0, other=True),
    }
    early = cross(middle | last, table)
    late = cross(first | middle | second, table, *early)
    home, away = gather(exchange(late))
    return finish(home, send(away, -1)).reshape(ROUNDS + 1, S_DEV, 1, LAGS)


def solution(mesh):
    return jax.shard_map(
        body,
        mesh=mesh,
        in_specs=(P(None, None, "pair", "band"), P(None, "pair")),
        out_specs=P(None, "pair", "band", None),
        check_vma=False,
    )
```

```python
import math

import jax
import jax.numpy as jnp
from jax import lax
from jax.experimental import pallas as pl
from jax.experimental.pallas import tpu as pltpu
from jax.sharding import PartitionSpec as P

WIN = 64
ROUNDS = 6
BAND_BINS = 128
LAGS = 128
NBINS = 2048
S_DEV = 8
LINES = 2 * WIN
GROUP = 8
GROUPS = BAND_BINS // GROUP
PIECE = S_DEV * GROUP
ROWS = 2 * PIECE
CHUNKS = 2
VMEM_LIMIT = 24 * 1024 * 1024


def core_index():
    return lax.rem(lax.axis_index("pair"), 2)


def whiten_kernel(spectra_hbm, valid_hbm, *refs):
    out_refs, (raw, valid, lines_ref, sems) = refs[:6], refs[6:]
    core = core_index()
    step = WIN // CHUNKS
    copies = []
    for chunk in range(CHUNKS):
        span = pl.ds(chunk * step, step)
        copies.append(
            pltpu.make_async_copy(spectra_hbm.at[:, span], raw.at[:, span], sems.at[chunk])
        )
        copies[-1].start()
    copies.append(pltpu.make_async_copy(valid_hbm, valid, sems.at[CHUNKS]))
    copies[-1].start()
    for chunk in range(CHUNKS):
        copies[chunk].wait()
        values = raw[:, chunk * step : (chunk + 1) * step].astype(jnp.float32)
        magnitude = jnp.sqrt(values[0] * values[0] + values[1] * values[1])
        for half in range(2):
            cut = slice(half * BAND_BINS, (half + 1) * BAND_BINS)
            band_mean = jnp.sum(magnitude[:, :, cut], axis=-1, keepdims=True) * (1.0 / BAND_BINS)
            factor = 1.0 / (band_mean + 1e-06)
            scaled = values[:, :, :, cut] * factor[None]
            for part in range(2):
                first = (part * WIN + chunk * step) * S_DEV
                lines_ref[half, first : first + step * S_DEV, :] = scaled[part].reshape(
                    step * S_DEV, BAND_BINS
                )
    copies[CHUNKS].wait()
    usable = valid[...].astype(jnp.float32)
    usable = jnp.concatenate([usable, usable], axis=1)
    for index, half in enumerate((core, 1 - core)):
        for pair in range(S_DEV // 2):
            parts = []
            for station in (2 * pair, 2 * pair + 1):
                lines = lines_ref[half, pl.ds(station, LINES, stride=S_DEV), :]
                turned = lines.T * usable[station : station + 1, :]
                parts.append(turned.reshape(GROUPS, GROUP, LINES))
            both = jnp.concatenate(parts, axis=1).astype(jnp.bfloat16)
            for out_ref in out_refs[index::2]:
                out_ref[:, pair * 2 * GROUP : (pair + 1) * 2 * GROUP, :] = both


def whiten(spectra, valid):
    piece = jax.ShapeDtypeStruct((GROUPS, PIECE, LINES), jnp.bfloat16)
    return pl.pallas_call(
        whiten_kernel,
        out_shape=(piece,) * 6,
        in_specs=[pl.BlockSpec(memory_space=pltpu.HBM)] * 2,
        out_specs=[pl.BlockSpec(memory_space=pltpu.VMEM)] * 6,
        scratch_shapes=[
            pltpu.VMEM((2, WIN, S_DEV, 2 * BAND_BINS), jnp.bfloat16),
            pltpu.VMEM((S_DEV, WIN), jnp.int32),
            pltpu.VMEM((2, LINES * S_DEV, BAND_BINS), jnp.float32),
            pltpu.SemaphoreType.DMA((CHUNKS + 1,)),
        ],
        compiler_params=pltpu.CompilerParams(vmem_limit_bytes=VMEM_LIMIT),
    )(
        pltpu.with_memory_space_constraint(spectra, pltpu.HBM),
        pltpu.with_memory_space_constraint(valid, pltpu.HBM),
    )


FAR, NEAR, OWN = 0, 1, 2


def cross_kernel(places, *refs):
    late = (FAR, 0) in places
    piece_refs = refs[: len(places)]
    if late:
        table_ref, early_ref, left, out_ref, held, turned, sems = refs[len(places) :]
        out_ref[:, :2] = early_ref[...]
    else:
        table_ref, out_ref, left, held, turned, sems = refs[len(places) :]
    core = core_index()
    copies = []
    for index, (chip, other) in enumerate(places):
        if late and chip != FAR:
            continue
        parity = 1 - core if other else core
        start = pl.multiple_of(parity * PIECE, PIECE)
        copy = pltpu.make_async_copy(
            piece_refs[index], held.at[chip, :, pl.ds(start, PIECE), :], sems.at[index]
        )
        copy.start()
        copies.append(copy)
    for copy in copies:
        copy.wait()
    pairs = ((OWN, FAR), (NEAR, FAR)) if late else ((OWN, OWN), (NEAR, OWN))

    row = lax.broadcasted_iota(jnp.int32, (ROWS, ROWS), 0)
    col = lax.broadcasted_iota(jnp.int32, (ROWS, ROWS), 1)
    swap_rows = (col == (row % 16) * GROUP + row // 16).astype(jnp.bfloat16)
    lane = lax.broadcasted_iota(jnp.int32, (16, ROWS), 1)
    sign = jnp.where(lax.broadcasted_iota(jnp.int32, (ROWS, LINES), 1) < WIN, -1.0, 1.0)

    for number, (p_side, q_side) in enumerate(() if late else pairs):
        for group in range(GROUPS):
            plain = jnp.dot(
                swap_rows, held[p_side, group], preferred_element_type=jnp.float32
            )
            flipped = pltpu.roll(plain, WIN, 1) * sign
            left[number, group, :ROWS, :] = plain.astype(jnp.bfloat16)
            left[number, group, ROWS:, :] = flipped.astype(jnp.bfloat16)

    for group in range(GROUPS):
        picked = []
        for number, (p_side, q_side) in enumerate(pairs):
            full = lax.dot_general(
                left[number, group],
                held[q_side, group],
                (((1,), (1,)), ((), ())),
                preferred_element_type=jnp.float32,
            )
            for part in range(2):
                total = jnp.zeros((16, ROWS), jnp.float32)
                for line in range(GROUP):
                    first = part * ROWS + line * 16
                    total = jnp.where(
                        lane % GROUP == line, full[first : first + 16, :], total
                    )
                picked.append(total)
        stacked = jnp.concatenate([picked[0], picked[2], picked[1], picked[3]], axis=0)
        turned[:, group * GROUP : (group + 1) * GROUP, :] = stacked.T.reshape(16, GROUP, 64)

    table_high = table_ref[...].astype(jnp.bfloat16)
    table_low = (table_ref[...] - table_high.astype(jnp.float32)).astype(jnp.bfloat16)
    for first_q in range(0, 8, 2):
        stations = (first_q, first_q + 8, first_q + 1, first_q + 9)
        lines = jnp.concatenate([turned[q].T for q in stations], axis=0)
        high = lines.astype(jnp.bfloat16)
        low = (lines - high.astype(jnp.float32)).astype(jnp.bfloat16)
        lagged = (
            jnp.dot(high, table_high, preferred_element_type=jnp.float32)
            + jnp.dot(low, table_high, preferred_element_type=jnp.float32)
            + jnp.dot(high, table_low, preferred_element_type=jnp.float32)
        )
        for step in range(2):
            sums = []
            for q_parity in range(2):
                part = lagged[(2 * step + q_parity) * 64 : (2 * step + q_parity + 1) * 64]
                sums.append(part[:32, :LAGS] + part[32:, LAGS:])
            for number in range(2):
                for parity in range(2):
                    cut = slice(number * 16 + parity * 8, number * 16 + parity * 8 + 8)
                    out_ref[parity * 8 + first_q + step, (2 if late else 0) + number] = (
                        jnp.concatenate([sums[0][cut], sums[1][cut]], axis=0).astype(
                            jnp.bfloat16
                        )
                    )


def cross(pieces, table, *early):
    places = tuple(pieces)
    shape = jax.ShapeDtypeStruct((16, 4 if early else 2, 16, LAGS), jnp.bfloat16)
    left = jax.ShapeDtypeStruct((2, GROUPS, 2 * ROWS, LINES), jnp.bfloat16)
    return pl.pallas_call(
        lambda *refs: cross_kernel(places, *refs),
        out_shape=shape if early else (shape, left),
        in_specs=[pl.BlockSpec(memory_space=pl.ANY)] * len(places)
        + [pl.BlockSpec(memory_space=pltpu.VMEM)] * (1 + len(early)),
        scratch_shapes=[
            pltpu.VMEM((3, GROUPS, ROWS, LINES), jnp.bfloat16),
            pltpu.VMEM((16, BAND_BINS, 64), jnp.float32),
            pltpu.SemaphoreType.DMA((len(places),)),
        ],
        compiler_params=pltpu.CompilerParams(vmem_limit_bytes=VMEM_LIMIT),
        cost_estimate=pl.CostEstimate(
            flops=2 * 2 * GROUPS * 3 * ROWS * ROWS * LINES,
            bytes_accessed=len(places) * 262144 + 262144,
            transcendentals=0,
        ),
    )(*pieces.values(), table, *early)


def gather_kernel(parts_ref, home_ref, away_ref):
    total = parts_ref[0].astype(jnp.float32)
    for index in range(1, 16):
        total = total + parts_ref[index].astype(jnp.float32)
    home_ref[0] = total[0]
    home_ref[1] = total[2]
    away_ref[0] = total[1]
    away_ref[1] = total[3]


def gather(parts):
    half = jax.ShapeDtypeStruct((2, 16, LAGS), jnp.float32)
    return pl.pallas_call(
        gather_kernel,
        out_shape=(half, half),
        compiler_params=pltpu.CompilerParams(vmem_limit_bytes=VMEM_LIMIT),
    )(parts)


def finish_kernel(home_ref, away_ref, out_ref, slots):
    core = core_index()
    band = lax.axis_index("band")
    scale = 1.0 / (math.sqrt(WIN) * math.sqrt(NBINS))
    slots[0:16] = home_ref[0]
    slots[16:32] = away_ref[0]
    slots[32:48] = home_ref[1]
    slots[48:64] = away_ref[1]
    for round_no in range(ROUNDS + 1):
        first = pl.multiple_of((round_no + core) * S_DEV, S_DEV)
        value = slots[pl.ds(first, S_DEV), :] * scale
        if round_no == 0:
            row = lax.broadcasted_iota(jnp.int32, (S_DEV, LAGS), 0)
            value = jnp.where(row == band, 0.0, value)
        out_ref[round_no] = value


def finish(home, away):
    return pl.pallas_call(
        finish_kernel,
        out_shape=jax.ShapeDtypeStruct((ROUNDS + 1, S_DEV, LAGS), jnp.float32),
        scratch_shapes=[pltpu.VMEM((8 * S_DEV, LAGS), jnp.float32)],
        compiler_params=pltpu.CompilerParams(vmem_limit_bytes=VMEM_LIMIT),
    )(home, away)


def send(value, chips, other=False):
    count = lax.axis_size("pair")
    pairs = []
    for source in range(count):
        target = source + 2 * chips
        if other:
            target = target + 1 - 2 * (source % 2)
        pairs.append((source, target % count))
    return lax.ppermute(value, "pair", pairs)


def exchange(value):
    bands = lax.axis_size("band")
    groups = [
        [(2 * chip + core) * bands + band for core in range(2) for band in range(bands)]
        for chip in range(lax.axis_size("pair") // 2)
    ]
    return lax.all_to_all(
        value, ("pair", "band"), 0, 0, tiled=True, axis_index_groups=groups
    )


def lag_table(first_bin):
    freq = first_bin + jnp.arange(BAND_BINS, dtype=jnp.int32)
    offsets = jnp.arange(LAGS, dtype=jnp.int32) - LAGS // 2
    wrapped = freq[:, None] * offsets[None, :] % (2 * NBINS)
    phase = math.pi * wrapped.astype(jnp.float32) / NBINS
    return jnp.concatenate([jnp.cos(phase), -jnp.sin(phase)], axis=1)


def body(spectra, validity):
    far_same, far_other, own_same, own_other, near_same, near_other = whiten(spectra, validity.T)
    first_bin = (lax.axis_index("band") * 2 + core_index()) * BAND_BINS
    table = lag_table(first_bin)
    first = {(FAR, 0): send(far_same, -2)}
    middle = {(NEAR, 0): send(near_same, 1)}
    second = {(FAR, 1): send(far_other, -2, other=True)}
    last = {
        (NEAR, 1): send(near_other, 1, other=True),
        (OWN, 0): own_same,
        (OWN, 1): send(own_other, 0, other=True),
    }
    early = cross(middle | last, table)
    late = cross(first | middle | second, table, *early)
    home, away = gather(exchange(late))
    return finish(home, send(away, -1)).reshape(ROUNDS + 1, S_DEV, 1, LAGS)


def solution(mesh):
    return jax.shard_map(
        body,
        mesh=mesh,
        in_specs=(P(None, None, "pair", "band"), P(None, "pair")),
        out_specs=P(None, "pair", "band", None),
        check_vma=False,
    )
```

```python
import math

import jax
import jax.numpy as jnp
from jax import lax
from jax.experimental import pallas as pl
from jax.experimental.pallas import tpu as pltpu
from jax.sharding import PartitionSpec as P

WIN = 64
ROUNDS = 6
BAND_BINS = 128
LAGS = 128
NBINS = 2048
S_DEV = 8
LINES = 2 * WIN
GROUP = 8
GROUPS = BAND_BINS // GROUP
PIECE = S_DEV * GROUP
ROWS = 2 * PIECE
CHUNKS = 2
VMEM_LIMIT = 24 * 1024 * 1024


def core_index():
    return lax.rem(lax.axis_index("pair"), 2)


def whiten_kernel(spectra_hbm, valid_hbm, *refs):
    out_refs, (raw, valid, lines_ref, sems) = refs[:6], refs[6:]
    core = core_index()
    step = WIN // CHUNKS
    copies = []
    for chunk in range(CHUNKS):
        span = pl.ds(chunk * step, step)
        copies.append(
            pltpu.make_async_copy(spectra_hbm.at[:, span], raw.at[:, span], sems.at[chunk])
        )
        copies[-1].start()
    copies.append(pltpu.make_async_copy(valid_hbm, valid, sems.at[CHUNKS]))
    copies[-1].start()
    for chunk in range(CHUNKS):
        copies[chunk].wait()
        values = raw[:, chunk * step : (chunk + 1) * step].astype(jnp.float32)
        magnitude = jnp.sqrt(values[0] * values[0] + values[1] * values[1])
        for half in range(2):
            cut = slice(half * BAND_BINS, (half + 1) * BAND_BINS)
            band_mean = jnp.sum(magnitude[:, :, cut], axis=-1, keepdims=True) * (1.0 / BAND_BINS)
            factor = 1.0 / (band_mean + 1e-06)
            scaled = values[:, :, :, cut] * factor[None]
            for part in range(2):
                first = (part * WIN + chunk * step) * S_DEV
                lines_ref[half, first : first + step * S_DEV, :] = scaled[part].reshape(
                    step * S_DEV, BAND_BINS
                )
    copies[CHUNKS].wait()
    usable = valid[...].astype(jnp.float32)
    usable = jnp.concatenate([usable, usable], axis=1)
    for index, half in enumerate((core, 1 - core)):
        for pair in range(S_DEV // 2):
            parts = []
            for station in (2 * pair, 2 * pair + 1):
                lines = lines_ref[half, pl.ds(station, LINES, stride=S_DEV), :]
                turned = lines.T * usable[station : station + 1, :]
                parts.append(turned.reshape(GROUPS, GROUP, LINES))
            both = jnp.concatenate(parts, axis=1).astype(jnp.bfloat16)
            for out_ref in out_refs[index::2]:
                out_ref[:, pair * 2 * GROUP : (pair + 1) * 2 * GROUP, :] = both


def whiten(spectra, valid):
    piece = jax.ShapeDtypeStruct((GROUPS, PIECE, LINES), jnp.bfloat16)
    return pl.pallas_call(
        whiten_kernel,
        out_shape=(piece,) * 6,
        in_specs=[pl.BlockSpec(memory_space=pltpu.HBM)] * 2,
        out_specs=[pl.BlockSpec(memory_space=pltpu.VMEM)] * 6,
        scratch_shapes=[
            pltpu.VMEM((2, WIN, S_DEV, 2 * BAND_BINS), jnp.bfloat16),
            pltpu.VMEM((S_DEV, WIN), jnp.int32),
            pltpu.VMEM((2, LINES * S_DEV, BAND_BINS), jnp.float32),
            pltpu.SemaphoreType.DMA((CHUNKS + 1,)),
        ],
        compiler_params=pltpu.CompilerParams(vmem_limit_bytes=VMEM_LIMIT),
    )(
        pltpu.with_memory_space_constraint(spectra, pltpu.HBM),
        pltpu.with_memory_space_constraint(valid, pltpu.HBM),
    )


FAR, NEAR, OWN = 0, 1, 2


def cross_kernel(places, *refs):
    late = (FAR, 0) in places
    piece_refs = refs[: len(places)]
    if late:
        table_ref, early_ref, left, out_ref, held, turned, sems = refs[len(places) :]
        out_ref[:, :2] = early_ref[...]
    else:
        table_ref, out_ref, left, held, turned, sems = refs[len(places) :]
    core = core_index()
    copies = []
    for index, (chip, other) in enumerate(places):
        if late and chip != FAR:
            continue
        parity = 1 - core if other else core
        start = pl.multiple_of(parity * PIECE, PIECE)
        copy = pltpu.make_async_copy(
            piece_refs[index], held.at[chip, :, pl.ds(start, PIECE), :], sems.at[index]
        )
        copy.start()
        copies.append(copy)
    for copy in copies:
        copy.wait()
    pairs = ((OWN, FAR), (NEAR, FAR)) if late else ((OWN, OWN), (NEAR, OWN))

    row = lax.broadcasted_iota(jnp.int32, (ROWS, ROWS), 0)
    col = lax.broadcasted_iota(jnp.int32, (ROWS, ROWS), 1)
    swap_rows = (col == (row % 16) * GROUP + row // 16).astype(jnp.bfloat16)
    lane = lax.broadcasted_iota(jnp.int32, (16, ROWS), 1)
    sign = jnp.where(lax.broadcasted_iota(jnp.int32, (ROWS, LINES), 1) < WIN, -1.0, 1.0)

    for number, (p_side, q_side) in enumerate(() if late else pairs):
        for group in range(GROUPS):
            plain = jnp.dot(
                swap_rows, held[p_side, group], preferred_element_type=jnp.float32
            )
            flipped = pltpu.roll(plain, WIN, 1) * sign
            left[number, group, :ROWS, :] = plain.astype(jnp.bfloat16)
            left[number, group, ROWS:, :] = flipped.astype(jnp.bfloat16)

    for group in range(GROUPS):
        picked = []
        for number, (p_side, q_side) in enumerate(pairs):
            full = lax.dot_general(
                left[number, group],
                held[q_side, group],
                (((1,), (1,)), ((), ())),
                preferred_element_type=jnp.float32,
            )
            for part in range(2):
                total = full[part * ROWS : part * ROWS + 16, :]
                for line in range(1, GROUP):
                    first = part * ROWS + line * 16
                    total = jnp.where(
                        lane % GROUP == line, full[first : first + 16, :], total
                    )
                picked.append(total)
        stacked = jnp.concatenate([picked[0], picked[2], picked[1], picked[3]], axis=0)
        turned[:, group * GROUP : (group + 1) * GROUP, :] = stacked.T.reshape(16, GROUP, 64)

    table_high = table_ref[...].astype(jnp.bfloat16)
    table_low = (table_ref[...] - table_high.astype(jnp.float32)).astype(jnp.bfloat16)
    for first_q in range(0, 8, 2):
        stations = (first_q, first_q + 8, first_q + 1, first_q + 9)
        lines = [turned[q].T for q in stations]
        lines = jnp.concatenate(
            [jnp.concatenate([line[part : part + 32] for line in lines], axis=0) for part in (0, 32)],
            axis=1,
        )
        high = lines.astype(jnp.bfloat16)
        low = (lines - high.astype(jnp.float32)).astype(jnp.bfloat16)
        lagged = (
            jnp.dot(high, table_high, preferred_element_type=jnp.float32)
            + jnp.dot(low, table_high, preferred_element_type=jnp.float32)
            + jnp.dot(high, table_low, preferred_element_type=jnp.float32)
        )
        for step in range(2):
            sums = []
            for q_parity in range(2):
                first = (2 * step + q_parity) * 32
                sums.append(lagged[first : first + 32])
            for number in range(2):
                for parity in range(2):
                    cut = slice(number * 16 + parity * 8, number * 16 + parity * 8 + 8)
                    out_ref[parity * 8 + first_q + step, (2 if late else 0) + number] = (
                        jnp.concatenate([sums[0][cut], sums[1][cut]], axis=0).astype(
                            jnp.bfloat16
                        )
                    )


def cross(pieces, table, *early):
    places = tuple(pieces)
    shape = jax.ShapeDtypeStruct((16, 4 if early else 2, 16, LAGS), jnp.bfloat16)
    left = jax.ShapeDtypeStruct((2, GROUPS, 2 * ROWS, LINES), jnp.bfloat16)
    return pl.pallas_call(
        lambda *refs: cross_kernel(places, *refs),
        out_shape=shape if early else (shape, left),
        in_specs=[pl.BlockSpec(memory_space=pl.ANY)] * len(places)
        + [pl.BlockSpec(memory_space=pltpu.VMEM)] * (1 + len(early)),
        scratch_shapes=[
            pltpu.VMEM((3, GROUPS, ROWS, LINES), jnp.bfloat16),
            pltpu.VMEM((16, BAND_BINS, 64), jnp.float32),
            pltpu.SemaphoreType.DMA((len(places),)),
        ],
        compiler_params=pltpu.CompilerParams(vmem_limit_bytes=VMEM_LIMIT),
        cost_estimate=pl.CostEstimate(
            flops=2 * 2 * GROUPS * 3 * ROWS * ROWS * LINES,
            bytes_accessed=len(places) * 262144 + 262144,
            transcendentals=0,
        ),
    )(*pieces.values(), table, *early)


def gather_kernel(parts_ref, home_ref, away_ref):
    total = parts_ref[0].astype(jnp.float32)
    for index in range(1, 16):
        total = total + parts_ref[index].astype(jnp.float32)
    home_ref[0] = total[0]
    home_ref[1] = total[2]
    away_ref[0] = total[1]
    away_ref[1] = total[3]


def gather(parts):
    half = jax.ShapeDtypeStruct((2, 16, LAGS), jnp.float32)
    return pl.pallas_call(
        gather_kernel,
        out_shape=(half, half),
        compiler_params=pltpu.CompilerParams(vmem_limit_bytes=VMEM_LIMIT),
    )(parts)


def finish_kernel(home_ref, away_ref, out_ref, slots):
    core = core_index()
    band = lax.axis_index("band")
    scale = 1.0 / (math.sqrt(WIN) * math.sqrt(NBINS))
    slots[0:16] = home_ref[0]
    slots[16:32] = away_ref[0]
    slots[32:48] = home_ref[1]
    slots[48:64] = away_ref[1]
    for round_no in range(ROUNDS + 1):
        first = pl.multiple_of((round_no + core) * S_DEV, S_DEV)
        value = slots[pl.ds(first, S_DEV), :] * scale
        if round_no == 0:
            row = lax.broadcasted_iota(jnp.int32, (S_DEV, LAGS), 0)
            value = jnp.where(row == band, 0.0, value)
        out_ref[round_no] = value


def finish(home, away):
    return pl.pallas_call(
        finish_kernel,
        out_shape=jax.ShapeDtypeStruct((ROUNDS + 1, S_DEV, LAGS), jnp.float32),
        scratch_shapes=[pltpu.VMEM((8 * S_DEV, LAGS), jnp.float32)],
        compiler_params=pltpu.CompilerParams(vmem_limit_bytes=VMEM_LIMIT),
    )(home, away)


def send(value, chips, other=False):
    count = lax.axis_size("pair")
    pairs = []
    for source in range(count):
        target = source + 2 * chips
        if other:
            target = target + 1 - 2 * (source % 2)
        pairs.append((source, target % count))
    return lax.ppermute(value, "pair", pairs)


def exchange(value):
    bands = lax.axis_size("band")
    groups = [
        [(2 * chip + core) * bands + band for core in range(2) for band in range(bands)]
        for chip in range(lax.axis_size("pair") // 2)
    ]
    return lax.all_to_all(
        value, ("pair", "band"), 0, 0, tiled=True, axis_index_groups=groups
    )


def lag_table(first_bin):
    freq = first_bin + jnp.arange(BAND_BINS, dtype=jnp.int32)
    offsets = jnp.arange(LAGS, dtype=jnp.int32) - LAGS // 2
    wrapped = freq[:, None] * offsets[None, :] % (2 * NBINS)
    phase = math.pi * wrapped.astype(jnp.float32) / NBINS
    return jnp.concatenate([jnp.cos(phase), -jnp.sin(phase)], axis=0)


def body(spectra, validity):
    far_same, far_other, own_same, own_other, near_same, near_other = whiten(spectra, validity.T)
    first_bin = (lax.axis_index("band") * 2 + core_index()) * BAND_BINS
    table = lag_table(first_bin)
    first = {(FAR, 0): send(far_same, -2)}
    middle = {(NEAR, 0): send(near_same, 1)}
    second = {(FAR, 1): send(far_other, -2, other=True)}
    last = {
        (NEAR, 1): send(near_other, 1, other=True),
        (OWN, 0): own_same,
        (OWN, 1): send(own_other, 0, other=True),
    }
    early = cross(middle | last, table)
    late = cross(first | middle | second, table, *early)
    home, away = gather(exchange(late))
    return finish(home, send(away, -1)).reshape(ROUNDS + 1, S_DEV, 1, LAGS)


def solution(mesh):
    return jax.shard_map(
        body,
        mesh=mesh,
        in_specs=(P(None, None, "pair", "band"), P(None, "pair")),
        out_specs=P(None, "pair", "band", None),
        check_vma=False,
    )
```

```python
import math

import jax
import jax.numpy as jnp
from jax import lax
from jax.experimental import pallas as pl
from jax.experimental.pallas import tpu as pltpu
from jax.sharding import PartitionSpec as P

WIN = 64
ROUNDS = 6
BAND_BINS = 128
LAGS = 128
NBINS = 2048
S_DEV = 8
LINES = 2 * WIN
GROUP = 8
GROUPS = BAND_BINS // GROUP
PIECE = S_DEV * GROUP
ROWS = 2 * PIECE
CHUNKS = 2
VMEM_LIMIT = 24 * 1024 * 1024


def core_index():
    return lax.rem(lax.axis_index("pair"), 2)


def whiten_kernel(spectra_hbm, valid_hbm, *refs):
    out_refs, (raw, valid, lines_ref, sems) = refs[:6], refs[6:]
    core = core_index()
    step = WIN // CHUNKS
    copies = []
    for chunk in range(CHUNKS):
        span = pl.ds(chunk * step, step)
        copies.append(
            pltpu.make_async_copy(spectra_hbm.at[:, span], raw.at[:, span], sems.at[chunk])
        )
        copies[-1].start()
    copies.append(pltpu.make_async_copy(valid_hbm, valid, sems.at[CHUNKS]))
    copies[-1].start()
    for chunk in range(CHUNKS):
        copies[chunk].wait()
        values = raw[:, chunk * step : (chunk + 1) * step].astype(jnp.float32)
        magnitude = jnp.sqrt(values[0] * values[0] + values[1] * values[1])
        for half in range(2):
            cut = slice(half * BAND_BINS, (half + 1) * BAND_BINS)
            band_mean = jnp.sum(magnitude[:, :, cut], axis=-1, keepdims=True) * (1.0 / BAND_BINS)
            factor = 1.0 / (band_mean + 1e-06)
            scaled = values[:, :, :, cut] * factor[None]
            for part in range(2):
                first = (part * WIN + chunk * step) * S_DEV
                lines_ref[half, first : first + step * S_DEV, :] = scaled[part].reshape(
                    step * S_DEV, BAND_BINS
                )
    copies[CHUNKS].wait()
    usable = valid[...].astype(jnp.float32)
    usable = jnp.concatenate([usable, usable], axis=1)
    for index, half in enumerate((core, 1 - core)):
        for pair in range(S_DEV // 2):
            parts = []
            for station in (2 * pair, 2 * pair + 1):
                lines = lines_ref[half, pl.ds(station, LINES, stride=S_DEV), :]
                turned = lines.T * usable[station : station + 1, :]
                parts.append(turned.reshape(GROUPS, GROUP, LINES))
            both = jnp.concatenate(parts, axis=1).astype(jnp.bfloat16)
            for out_ref in out_refs[index::2]:
                out_ref[:, pair * 2 * GROUP : (pair + 1) * 2 * GROUP, :] = both


def whiten(spectra, valid):
    piece = jax.ShapeDtypeStruct((GROUPS, PIECE, LINES), jnp.bfloat16)
    return pl.pallas_call(
        whiten_kernel,
        out_shape=(piece,) * 6,
        in_specs=[pl.BlockSpec(memory_space=pltpu.HBM)] * 2,
        out_specs=[pl.BlockSpec(memory_space=pltpu.VMEM)] * 6,
        scratch_shapes=[
            pltpu.VMEM((2, WIN, S_DEV, 2 * BAND_BINS), jnp.bfloat16),
            pltpu.VMEM((S_DEV, WIN), jnp.int32),
            pltpu.VMEM((2, LINES * S_DEV, BAND_BINS), jnp.float32),
            pltpu.SemaphoreType.DMA((CHUNKS + 1,)),
        ],
        compiler_params=pltpu.CompilerParams(vmem_limit_bytes=VMEM_LIMIT),
    )(
        pltpu.with_memory_space_constraint(spectra, pltpu.HBM),
        pltpu.with_memory_space_constraint(valid, pltpu.HBM),
    )


FAR, NEAR, OWN = 0, 1, 2


def cross_kernel(places, *refs):
    late = (FAR, 0) in places
    piece_refs = refs[: len(places)]
    if late:
        table_ref, early_ref, left, out_ref, held, turned, sems = refs[len(places) :]
        out_ref[:, :2] = early_ref[...]
    else:
        table_ref, out_ref, left, held, turned, sems = refs[len(places) :]
    core = core_index()
    copies = []
    for index, (chip, other) in enumerate(places):
        if late:
            continue
        parity = 1 - core if other else core
        start = pl.multiple_of(parity * PIECE, PIECE)
        copy = pltpu.make_async_copy(
            piece_refs[index], held.at[chip, :, pl.ds(start, PIECE), :], sems.at[index]
        )
        copy.start()
        copies.append(copy)
    for copy in copies:
        copy.wait()
    pairs = ((OWN, FAR), (NEAR, FAR)) if late else ((OWN, OWN), (NEAR, OWN))

    row = lax.broadcasted_iota(jnp.int32, (ROWS, ROWS), 0)
    col = lax.broadcasted_iota(jnp.int32, (ROWS, ROWS), 1)
    swap_rows = (col == (row % 16) * GROUP + row // 16).astype(jnp.bfloat16)
    lane = lax.broadcasted_iota(jnp.int32, (16, ROWS), 1)
    sign = jnp.where(lax.broadcasted_iota(jnp.int32, (ROWS, LINES), 1) < WIN, -1.0, 1.0)

    for number, (p_side, q_side) in enumerate(() if late else pairs):
        for group in range(GROUPS):
            plain = jnp.dot(
                swap_rows, held[p_side, group], preferred_element_type=jnp.float32
            )
            flipped = pltpu.roll(plain, WIN, 1) * sign
            left[number, group, :ROWS, :] = plain.astype(jnp.bfloat16)
            left[number, group, ROWS:, :] = flipped.astype(jnp.bfloat16)

    for group in range(GROUPS):
        picked = []
        if late:
            mine = piece_refs[places.index((FAR, 0))][group]
            others = piece_refs[places.index((FAR, 1))][group]
            right = jnp.concatenate(
                [jnp.where(core == 0, mine, others), jnp.where(core == 0, others, mine)], axis=0
            )
        else:
            right = held[OWN, group]
        for number, (p_side, q_side) in enumerate(pairs):
            full = lax.dot_general(
                left[number, group],
                right,
                (((1,), (1,)), ((), ())),
                preferred_element_type=jnp.float32,
            )
            for part in range(2):
                total = full[part * ROWS : part * ROWS + 16, :]
                for line in range(1, GROUP):
                    first = part * ROWS + line * 16
                    total = jnp.where(
                        lane % GROUP == line, full[first : first + 16, :], total
                    )
                picked.append(total)
        stacked = jnp.concatenate([picked[0], picked[2], picked[1], picked[3]], axis=0)
        turned[:, group * GROUP : (group + 1) * GROUP, :] = stacked.T.reshape(16, GROUP, 64)

    table_high = table_ref[...].astype(jnp.bfloat16)
    table_low = (table_ref[...] - table_high.astype(jnp.float32)).astype(jnp.bfloat16)
    for first_q in range(0, 8, 2):
        stations = (first_q, first_q + 8, first_q + 1, first_q + 9)
        lines = [turned[q].T for q in stations]
        lines = jnp.concatenate(
            [jnp.concatenate([line[part : part + 32] for line in lines], axis=0) for part in (0, 32)],
            axis=1,
        )
        high = lines.astype(jnp.bfloat16)
        low = (lines - high.astype(jnp.float32)).astype(jnp.bfloat16)
        lagged = (
            jnp.dot(high, table_high, preferred_element_type=jnp.float32)
            + jnp.dot(low, table_high, preferred_element_type=jnp.float32)
            + jnp.dot(high, table_low, preferred_element_type=jnp.float32)
        )
        for step in range(2):
            sums = []
            for q_parity in range(2):
                first = (2 * step + q_parity) * 32
                sums.append(lagged[first : first + 32])
            for number in range(2):
                for parity in range(2):
                    cut = slice(number * 16 + parity * 8, number * 16 + parity * 8 + 8)
                    out_ref[parity * 8 + first_q + step, (2 if late else 0) + number] = (
                        jnp.concatenate([sums[0][cut], sums[1][cut]], axis=0).astype(
                            jnp.bfloat16
                        )
                    )


def cross(pieces, table, *early):
    places = tuple(pieces)
    shape = jax.ShapeDtypeStruct((16, 4 if early else 2, 16, LAGS), jnp.bfloat16)
    left = jax.ShapeDtypeStruct((2, GROUPS, 2 * ROWS, LINES), jnp.bfloat16)
    return pl.pallas_call(
        lambda *refs: cross_kernel(places, *refs),
        out_shape=shape if early else (shape, left),
        in_specs=[
            pl.BlockSpec(memory_space=pltpu.VMEM if early and chip == FAR else pl.ANY)
            for chip, _ in places
        ]
        + [pl.BlockSpec(memory_space=pltpu.VMEM)] * (1 + len(early)),
        scratch_shapes=[
            pltpu.VMEM((3, GROUPS, ROWS, LINES), jnp.bfloat16),
            pltpu.VMEM((16, BAND_BINS, 64), jnp.float32),
            pltpu.SemaphoreType.DMA((len(places),)),
        ],
        compiler_params=pltpu.CompilerParams(vmem_limit_bytes=VMEM_LIMIT),
        cost_estimate=pl.CostEstimate(
            flops=2 * 2 * GROUPS * 3 * ROWS * ROWS * LINES,
            bytes_accessed=len(places) * 262144 + 262144,
            transcendentals=0,
        ),
    )(*pieces.values(), table, *early)


def gather_kernel(parts_ref, home_ref, away_ref):
    total = parts_ref[0].astype(jnp.float32)
    for index in range(1, 16):
        total = total + parts_ref[index].astype(jnp.float32)
    home_ref[0] = total[0]
    home_ref[1] = total[2]
    away_ref[0] = total[1]
    away_ref[1] = total[3]


def gather(parts):
    half = jax.ShapeDtypeStruct((2, 16, LAGS), jnp.float32)
    return pl.pallas_call(
        gather_kernel,
        out_shape=(half, half),
        compiler_params=pltpu.CompilerParams(vmem_limit_bytes=VMEM_LIMIT),
    )(parts)


def finish_kernel(home_ref, away_ref, out_ref, slots):
    core = core_index()
    band = lax.axis_index("band")
    scale = 1.0 / (math.sqrt(WIN) * math.sqrt(NBINS))
    slots[0:16] = home_ref[0]
    slots[16:32] = away_ref[0]
    slots[32:48] = home_ref[1]
    slots[48:64] = away_ref[1]
    for round_no in range(ROUNDS + 1):
        first = pl.multiple_of((round_no + core) * S_DEV, S_DEV)
        value = slots[pl.ds(first, S_DEV), :] * scale
        if round_no == 0:
            row = lax.broadcasted_iota(jnp.int32, (S_DEV, LAGS), 0)
            value = jnp.where(row == band, 0.0, value)
        out_ref[round_no] = value


def finish(home, away):
    return pl.pallas_call(
        finish_kernel,
        out_shape=jax.ShapeDtypeStruct((ROUNDS + 1, S_DEV, LAGS), jnp.float32),
        scratch_shapes=[pltpu.VMEM((8 * S_DEV, LAGS), jnp.float32)],
        compiler_params=pltpu.CompilerParams(vmem_limit_bytes=VMEM_LIMIT),
    )(home, away)


def send(value, chips, other=False):
    count = lax.axis_size("pair")
    pairs = []
    for source in range(count):
        target = source + 2 * chips
        if other:
            target = target + 1 - 2 * (source % 2)
        pairs.append((source, target % count))
    return lax.ppermute(value, "pair", pairs)


def exchange(value):
    bands = lax.axis_size("band")
    groups = [
        [(2 * chip + core) * bands + band for core in range(2) for band in range(bands)]
        for chip in range(lax.axis_size("pair") // 2)
    ]
    return lax.all_to_all(
        value, ("pair", "band"), 0, 0, tiled=True, axis_index_groups=groups
    )


def lag_table(first_bin):
    freq = first_bin + jnp.arange(BAND_BINS, dtype=jnp.int32)
    offsets = jnp.arange(LAGS, dtype=jnp.int32) - LAGS // 2
    wrapped = freq[:, None] * offsets[None, :] % (2 * NBINS)
    phase = math.pi * wrapped.astype(jnp.float32) / NBINS
    return jnp.concatenate([jnp.cos(phase), -jnp.sin(phase)], axis=0)


def body(spectra, validity):
    far_same, far_other, own_same, own_other, near_same, near_other = whiten(spectra, validity.T)
    first_bin = (lax.axis_index("band") * 2 + core_index()) * BAND_BINS
    table = lag_table(first_bin)
    first = {(FAR, 0): send(far_same, -2)}
    middle = {(NEAR, 0): send(near_same, 1)}
    second = {(FAR, 1): send(far_other, -2, other=True)}
    last = {
        (NEAR, 1): send(near_other, 1, other=True),
        (OWN, 0): own_same,
        (OWN, 1): send(own_other, 0, other=True),
    }
    early = cross(middle | last, table)
    late = cross(first | middle | second, table, *early)
    home, away = gather(exchange(late))
    return finish(home, send(away, -1)).reshape(ROUNDS + 1, S_DEV, 1, LAGS)


def solution(mesh):
    return jax.shard_map(
        body,
        mesh=mesh,
        in_specs=(P(None, None, "pair", "band"), P(None, "pair")),
        out_specs=P(None, "pair", "band", None),
        check_vma=False,
    )
```

```python
import math

import jax
import jax.numpy as jnp
from jax import lax
from jax.experimental import pallas as pl
from jax.experimental.pallas import tpu as pltpu
from jax.sharding import PartitionSpec as P

WIN = 64
ROUNDS = 6
BAND_BINS = 128
LAGS = 128
NBINS = 2048
S_DEV = 8
LINES = 2 * WIN
GROUP = 8
GROUPS = BAND_BINS // GROUP
PIECE = S_DEV * GROUP
ROWS = 2 * PIECE
CHUNKS = 2
VMEM_LIMIT = 24 * 1024 * 1024


def core_index():
    return lax.rem(lax.axis_index("pair"), 2)


def whiten_kernel(spectra_hbm, valid_hbm, *refs):
    out_refs, (raw, valid, lines_ref, sems) = refs[:6], refs[6:]
    core = core_index()
    step = WIN // CHUNKS
    copies = []
    for chunk in range(CHUNKS):
        span = pl.ds(chunk * step, step)
        copies.append(
            pltpu.make_async_copy(spectra_hbm.at[:, span], raw.at[:, span], sems.at[chunk])
        )
        copies[-1].start()
    copies.append(pltpu.make_async_copy(valid_hbm, valid, sems.at[CHUNKS]))
    copies[-1].start()
    for chunk in range(CHUNKS):
        copies[chunk].wait()
        values = raw[:, chunk * step : (chunk + 1) * step].astype(jnp.float32)
        magnitude = jnp.sqrt(values[0] * values[0] + values[1] * values[1])
        for half in range(2):
            cut = slice(half * BAND_BINS, (half + 1) * BAND_BINS)
            band_mean = jnp.sum(magnitude[:, :, cut], axis=-1, keepdims=True) * (1.0 / BAND_BINS)
            factor = 1.0 / (band_mean + 1e-06)
            scaled = values[:, :, :, cut] * factor[None]
            for part in range(2):
                first = (part * WIN + chunk * step) * S_DEV
                lines_ref[half, first : first + step * S_DEV, :] = scaled[part].reshape(
                    step * S_DEV, BAND_BINS
                )
    copies[CHUNKS].wait()
    usable = valid[...].astype(jnp.float32)
    usable = jnp.concatenate([usable, usable], axis=1)
    for index, half in enumerate((core, 1 - core)):
        for pair in range(S_DEV // 2):
            parts = []
            for station in (2 * pair, 2 * pair + 1):
                lines = lines_ref[half, pl.ds(station, LINES, stride=S_DEV), :]
                turned = lines.T * usable[station : station + 1, :]
                parts.append(turned.reshape(GROUPS, GROUP, LINES))
            both = jnp.concatenate(parts, axis=1).astype(jnp.bfloat16)
            for out_ref in out_refs[index::2]:
                out_ref[:, pair * 2 * GROUP : (pair + 1) * 2 * GROUP, :] = both


def whiten(spectra, valid):
    piece = jax.ShapeDtypeStruct((GROUPS, PIECE, LINES), jnp.bfloat16)
    return pl.pallas_call(
        whiten_kernel,
        out_shape=(piece,) * 6,
        in_specs=[pl.BlockSpec(memory_space=pltpu.HBM)] * 2,
        out_specs=[pl.BlockSpec(memory_space=pltpu.VMEM)] * 6,
        scratch_shapes=[
            pltpu.VMEM((2, WIN, S_DEV, 2 * BAND_BINS), jnp.bfloat16),
            pltpu.VMEM((S_DEV, WIN), jnp.int32),
            pltpu.VMEM((2, LINES * S_DEV, BAND_BINS), jnp.float32),
            pltpu.SemaphoreType.DMA((CHUNKS + 1,)),
        ],
        compiler_params=pltpu.CompilerParams(vmem_limit_bytes=VMEM_LIMIT),
    )(
        pltpu.with_memory_space_constraint(spectra, pltpu.HBM),
        pltpu.with_memory_space_constraint(valid, pltpu.HBM),
    )


FAR, NEAR, OWN = 0, 1, 2


def cross_kernel(places, *refs):
    late = (FAR, 0) in places
    piece_refs = refs[: len(places)]
    if late:
        table_ref, early_ref, left, out_ref, held, turned, sems = refs[len(places) :]
        out_ref[:, :2] = early_ref[...]
    else:
        table_ref, out_ref, left, held, turned, sems = refs[len(places) :]
    core = core_index()
    copies = []
    for index, (chip, other) in enumerate(places):
        if late and chip != FAR:
            continue
        parity = 1 - core if other else core
        start = pl.multiple_of(parity * PIECE, PIECE)
        copy = pltpu.make_async_copy(
            piece_refs[index], held.at[chip, :, pl.ds(start, PIECE), :], sems.at[index]
        )
        copy.start()
        copies.append(copy)
    for copy in copies:
        copy.wait()
    pairs = ((OWN, FAR), (NEAR, FAR)) if late else ((OWN, OWN), (NEAR, OWN))

    row = lax.broadcasted_iota(jnp.int32, (ROWS, ROWS), 0)
    col = lax.broadcasted_iota(jnp.int32, (ROWS, ROWS), 1)
    swap_rows = (col == (row % 16) * GROUP + row // 16).astype(jnp.bfloat16)
    lane = lax.broadcasted_iota(jnp.int32, (16, ROWS), 1)
    sign = jnp.where(lax.broadcasted_iota(jnp.int32, (ROWS, LINES), 1) < WIN, -1.0, 1.0)

    for number, (p_side, q_side) in enumerate(() if late else pairs):
        for group in range(GROUPS):
            plain = jnp.dot(
                swap_rows, held[p_side, group], preferred_element_type=jnp.float32
            )
            flipped = pltpu.roll(plain, WIN, 1) * sign
            left[number, group, :ROWS, :] = plain.astype(jnp.bfloat16)
            left[number, group, ROWS:, :] = flipped.astype(jnp.bfloat16)

    for group in range(GROUPS):
        picked = []
        for number, (p_side, q_side) in enumerate(pairs):
            full = lax.dot_general(
                left[number, group],
                held[q_side, group],
                (((1,), (1,)), ((), ())),
                preferred_element_type=jnp.float32,
            )
            for part in range(2):
                total = full[part * ROWS : part * ROWS + 16, :]
                for line in range(1, GROUP):
                    first = part * ROWS + line * 16
                    total = jnp.where(
                        lane % GROUP == line, full[first : first + 16, :], total
                    )
                picked.append(total)
        stacked = jnp.concatenate([picked[0], picked[2], picked[1], picked[3]], axis=0)
        turned[:, group * GROUP : (group + 1) * GROUP, :] = stacked.T.reshape(16, GROUP, 64)

    table_high = table_ref[...].astype(jnp.bfloat16)
    table_low = (table_ref[...] - table_high.astype(jnp.float32)).astype(jnp.bfloat16)
    for first_q in range(0, 8, 2):
        stations = (first_q, first_q + 8, first_q + 1, first_q + 9)
        lines = [turned[q].T for q in stations]
        lines = jnp.concatenate(
            [jnp.concatenate([line[part : part + 32] for line in lines], axis=0) for part in (0, 32)],
            axis=1,
        )
        high = lines.astype(jnp.bfloat16)
        low = (lines - high.astype(jnp.float32)).astype(jnp.bfloat16)
        lagged = (
            jnp.dot(high, table_high, preferred_element_type=jnp.float32)
            + jnp.dot(low, table_high, preferred_element_type=jnp.float32)
            + jnp.dot(high, table_low, preferred_element_type=jnp.float32)
        )
        for step in range(2):
            sums = []
            for q_parity in range(2):
                first = (2 * step + q_parity) * 32
                sums.append(lagged[first : first + 32])
            for number in range(2):
                for parity in range(2):
                    cut = slice(number * 16 + parity * 8, number * 16 + parity * 8 + 8)
                    out_ref[(first_q + step) * 2 + parity, (2 if late else 0) + number] = (
                        jnp.concatenate([sums[0][cut], sums[1][cut]], axis=0).astype(
                            jnp.bfloat16
                        )
                    )


def cross(pieces, table, *early):
    places = tuple(pieces)
    shape = jax.ShapeDtypeStruct((16, 4 if early else 2, 16, LAGS), jnp.bfloat16)
    left = jax.ShapeDtypeStruct((2, GROUPS, 2 * ROWS, LINES), jnp.bfloat16)
    return pl.pallas_call(
        lambda *refs: cross_kernel(places, *refs),
        out_shape=shape if early else (shape, left),
        in_specs=[pl.BlockSpec(memory_space=pl.ANY)] * len(places)
        + [pl.BlockSpec(memory_space=pltpu.VMEM)] * (1 + len(early)),
        scratch_shapes=[
            pltpu.VMEM((3, GROUPS, ROWS, LINES), jnp.bfloat16),
            pltpu.VMEM((16, BAND_BINS, 64), jnp.float32),
            pltpu.SemaphoreType.DMA((len(places),)),
        ],
        compiler_params=pltpu.CompilerParams(vmem_limit_bytes=VMEM_LIMIT),
        cost_estimate=pl.CostEstimate(
            flops=2 * 2 * GROUPS * 3 * ROWS * ROWS * LINES,
            bytes_accessed=len(places) * 262144 + 262144,
            transcendentals=0,
        ),
    )(*pieces.values(), table, *early)


def gather_kernel(parts_ref, home_ref, away_ref):
    total = parts_ref[0].astype(jnp.float32)
    for index in range(1, 16):
        total = total + parts_ref[index].astype(jnp.float32)
    home_ref[0] = total[0]
    home_ref[1] = total[2]
    away_ref[0] = total[1]
    away_ref[1] = total[3]


def gather(parts):
    half = jax.ShapeDtypeStruct((2, 16, LAGS), jnp.float32)
    return pl.pallas_call(
        gather_kernel,
        out_shape=(half, half),
        compiler_params=pltpu.CompilerParams(vmem_limit_bytes=VMEM_LIMIT),
    )(parts)


def finish_kernel(home_ref, away_ref, out_ref, slots):
    core = core_index()
    band = lax.axis_index("band")
    scale = 1.0 / (math.sqrt(WIN) * math.sqrt(NBINS))
    slots[0:16] = home_ref[0]
    slots[16:32] = away_ref[0]
    slots[32:48] = home_ref[1]
    slots[48:64] = away_ref[1]
    for round_no in range(ROUNDS + 1):
        first = pl.multiple_of((round_no + core) * S_DEV, S_DEV)
        value = slots[pl.ds(first, S_DEV), :] * scale
        if round_no == 0:
            row = lax.broadcasted_iota(jnp.int32, (S_DEV, LAGS), 0)
            value = jnp.where(row == band, 0.0, value)
        out_ref[round_no] = value


def finish(home, away):
    return pl.pallas_call(
        finish_kernel,
        out_shape=jax.ShapeDtypeStruct((ROUNDS + 1, S_DEV, LAGS), jnp.float32),
        scratch_shapes=[pltpu.VMEM((8 * S_DEV, LAGS), jnp.float32)],
        compiler_params=pltpu.CompilerParams(vmem_limit_bytes=VMEM_LIMIT),
    )(home, away)


def send(value, chips, other=False):
    count = lax.axis_size("pair")
    pairs = []
    for source in range(count):
        target = source + 2 * chips
        if other:
            target = target + 1 - 2 * (source % 2)
        pairs.append((source, target % count))
    return lax.ppermute(value, "pair", pairs)


def exchange(value):
    bands = lax.axis_size("band")
    groups = [
        [(2 * chip + core) * bands + band for band in range(bands) for core in range(2)]
        for chip in range(lax.axis_size("pair") // 2)
    ]
    return lax.all_to_all(
        value, ("pair", "band"), 0, 0, tiled=True, axis_index_groups=groups
    )


def lag_table(first_bin):
    freq = first_bin + jnp.arange(BAND_BINS, dtype=jnp.int32)
    offsets = jnp.arange(LAGS, dtype=jnp.int32) - LAGS // 2
    wrapped = freq[:, None] * offsets[None, :] % (2 * NBINS)
    phase = math.pi * wrapped.astype(jnp.float32) / NBINS
    return jnp.concatenate([jnp.cos(phase), -jnp.sin(phase)], axis=0)


def body(spectra, validity):
    far_same, far_other, own_same, own_other, near_same, near_other = whiten(spectra, validity.T)
    first_bin = (lax.axis_index("band") * 2 + core_index()) * BAND_BINS
    table = lag_table(first_bin)
    first = {(FAR, 0): send(far_same, -2)}
    middle = {(NEAR, 0): send(near_same, 1)}
    second = {(FAR, 1): send(far_other, -2, other=True)}
    last = {
        (NEAR, 1): send(near_other, 1, other=True),
        (OWN, 0): own_same,
        (OWN, 1): send(own_other, 0, other=True),
    }
    early = cross(middle | last, table)
    late = cross(first | middle | second, table, *early)
    home, away = gather(exchange(late))
    return finish(home, send(away, -1)).reshape(ROUNDS + 1, S_DEV, 1, LAGS)


def solution(mesh):
    return jax.shard_map(
        body,
        mesh=mesh,
        in_specs=(P(None, None, "pair", "band"), P(None, "pair")),
        out_specs=P(None, "pair", "band", None),
        check_vma=False,
    )
```
